32 devices in a mesh: seg: 16 (over z, y, x), sub: 2 (over core).
Axes of the slice: x: 2, y: 2, z: 4, core: 2. Of those that a mesh axis runs over, the one named last changes fastest.
Arguments:
- start_field: float32 [3, 221184], P(None, ('seg', 'sub')), may hold values from -6 to 6
- element_loads: float32 [192, 8192], P(None, ('seg', 'sub')), may hold values from -6 to 6
- element_coefs: float32 [2, 8192], P(None, ('seg', 'sub')), may hold values from 0.2 to 5
- element_nodes: int32 [64, 8192], P(None, ('seg', 'sub')), may hold values from 0 to 7295, as said below
- move_list: int32 [3, 8192], P(None, ('seg', 'sub')), may hold values from 0 to 255, as said below
- face_nodes: int32 [2, 6144], P(None, ('seg', 'sub')), may hold values from 0 to 6911, as said below
- stiffness: float32 [2, 192, 192], replicated, as said below
Outputs:
- smoothed: float32 [3, 221184], P(None, ('seg', 'sub'))
- moved_loads: float32 [192, 8192], P(None, ('seg', 'sub'))
- moved_coefs: float32 [2, 8192], P(None, ('seg', 'sub'))
The draws below stay inside these ranges and needn't reach their ends.
Inputs may be any that keep to these rules, and one draw needn't show every extreme that they name: `move_list`: column e describes the record in slot e of its device before migration: row 0 its destination device p, row 1 its slot there, row 2 its place in the list that its device sends to p. A record that stays keeps its slot and has place 0. Every slot after migration receives exactly one record. A record leaves only for the device just before or after its own, with at most 16 records from one device to each and places below 16, or for a device two or more positions away, with at most 1 records from one device to one such device and places below 1; places are distinct for one source and destination. Both bounds are reached. `element_nodes`: column e lists the nodes of the element in slot e after migration in its device's numbering: values below 6912 are the device's own nodes, 6912 + s is entry s of face_nodes row 1 of the device before, 7104 + s entry s of face_nodes row 0 of the device after. The nodes of one element are distinct, every own node belongs to some element, the first device refers to no device before it and the last to none after it. `face_nodes`: for each device, row 0 lists own nodes that the device before refers to and row 1 those that the device after refers to; the 384 entries of one device are distinct. `stiffness`: both blocks are symmetric with positive diagonals and strictly diagonally dominant rows.
All inputs are finite; a program needn't handle non-finite values.
Results may differ from the reference program's by a relative error of at most 0.0001.
Values sent between devices are 32-bit elements; how exact they have to be, the bound alone decides.
A program may use at most 128 MiB of HBM per device.

```python
import math
import jax
import jax.numpy as jnp
from jax import lax

ELEM_NODES = 64
DOFS = 192
ELEM_DEV = 256
NODE_DEV = 6912
FACE = 192
NEAR_CAP = 16
FAR_CAP = 1
DEGREE = 4
SWEEPS = 2
ELEMENTS = 8192
NODES = 221184


def draw_element_nodes(key, part):
    devices = ELEMENTS // ELEM_DEV
    key_order, key_mult, key_turn, key_shuffle = jax.random.split(jax.random.fold_in(key, 101), 4)
    orders = jax.vmap(lambda one_key: jax.random.permutation(one_key, NODE_DEV))(jax.random.split(key_order, devices)).astype(jnp.int32)
    element = jnp.arange(ELEM_DEV, dtype=jnp.int32)[None, None, :]
    offset = jnp.arange(ELEM_NODES, dtype=jnp.int32)[None, :, None]
    device = jnp.arange(devices, dtype=jnp.int32)[:, None, None]
    position = (27 * element + offset) % NODE_DEV
    own_nodes = jnp.take(orders, position[0], axis=1)
    rim_count = FACE // 16
    back_use = (offset < 16) & (element < rim_count) & (device > 0)
    back_node = NODE_DEV + 16 * element + offset
    ahead_use = (offset >= ELEM_NODES - 16) & (element >= ELEM_DEV - rim_count) & (device < devices - 1)
    ahead_node = NODE_DEV + FACE + 16 * (element - (ELEM_DEV - rim_count)) + offset - (ELEM_NODES - 16)
    window = jnp.where(back_use, back_node, jnp.where(ahead_use, ahead_node, own_nodes))
    multiplier = 2 * jax.random.randint(key_mult, (devices, 1, ELEM_DEV), 0, ELEM_NODES // 2) + 1
    rotation = jax.random.randint(key_turn, (devices, 1, ELEM_DEV), 0, ELEM_NODES)
    chosen = (offset * multiplier + rotation) % ELEM_NODES
    result = jnp.take_along_axis(window, chosen, axis=1)
    shuffle = jax.vmap(lambda one_key: jax.random.permutation(one_key, ELEM_DEV))(jax.random.split(key_shuffle, devices)).astype(jnp.int32)
    result = jnp.take_along_axis(result, shuffle[:, None, :], axis=2)
    return result.transpose(1, 0, 2).reshape(ELEM_NODES, ELEMENTS).astype(jnp.int32)


def draw_move_list(key, part):
    devices = ELEMENTS // ELEM_DEV
    key_near, key_peak, key_far, key_full, key_spot, key_amount = jax.random.split(jax.random.fold_in(key, 202), 6)
    levels = jax.random.randint(key_near, (devices - 1,), 0, 5)
    boundary = jnp.maximum(jnp.right_shift(jnp.full((devices - 1,), NEAR_CAP, jnp.int32), levels), 1)
    peak_index = jax.random.randint(key_peak, (), 0, devices - 1)
    boundary = boundary.at[peak_index].set(NEAR_CAP)
    middle = ELEM_DEV - 2 * NEAR_CAP
    layout = jax.vmap(lambda one_key: jax.random.permutation(one_key, middle))(jax.random.split(key_spot, devices)).astype(jnp.int32)
    position = jnp.argsort(layout, axis=1).astype(jnp.int32)
    device_row = jnp.arange(devices, dtype=jnp.int32)
    upper = device_row[:, None] < device_row[None, :]
    pick = jax.random.randint(key_far, (devices, devices), 0, 10)
    amount = jax.random.randint(key_amount, (devices, devices), 1, FAR_CAP + 1)
    pick_sym = jnp.where(upper, pick, pick.T)
    amount_sym = jnp.where(upper, amount, amount.T)
    counts = jnp.where(pick_sym == 0, amount_sym, 0)
    target = jax.random.randint(key_full, (), 0, devices)
    full_mark = (device_row[:, None] == target) | (device_row[None, :] == target)
    counts = jnp.where(full_mark, FAR_CAP, counts)
    slot = jnp.arange(ELEM_DEV, dtype=jnp.int32)[None, :]
    device = device_row[:, None]
    zero_one = jnp.zeros((1,), jnp.int32)
    tail_count = jnp.concatenate([boundary, zero_one])[device]
    head_count = jnp.concatenate([zero_one, boundary])[device]
    tail_move = slot >= ELEM_DEV - tail_count
    head_move = slot < head_count
    tail_place = slot - (ELEM_DEV - tail_count)
    in_middle = (slot >= NEAR_CAP) & (slot < ELEM_DEV - NEAR_CAP)
    middle_index = jnp.broadcast_to(jnp.clip(slot - NEAR_CAP, 0, middle - 1), (devices, ELEM_DEV))
    region = jnp.where(in_middle, jnp.take_along_axis(layout, middle_index, axis=1), devices * FAR_CAP)
    partner = region // FAR_CAP
    inner = region % FAR_CAP
    partner_safe = jnp.clip(partner, 0, devices - 1)
    far_move = in_middle & (partner < devices) & (jnp.abs(partner - device) >= 2) & (inner < counts[device, partner_safe])
    far_index = jnp.clip(device * FAR_CAP + inner, 0, middle - 1)
    far_slot = NEAR_CAP + position[partner_safe, far_index]
    target_device = jnp.where(tail_move, device + 1, jnp.where(head_move, device - 1, jnp.where(far_move, partner_safe, device)))
    target_slot = jnp.where(tail_move, tail_place, jnp.where(head_move, ELEM_DEV - head_count + slot, jnp.where(far_move, far_slot, slot)))
    list_place = jnp.where(tail_move, tail_place, jnp.where(head_move, slot, jnp.where(far_move, inner, 0)))
    stacked = jnp.stack([target_device * jnp.ones_like(slot), target_slot, list_place])
    return stacked.reshape(3, ELEMENTS).astype(jnp.int32)


def draw_face_nodes(key, part):
    devices = ELEMENTS // ELEM_DEV
    key_pick, key_mix = jax.random.split(jax.random.fold_in(key, 303), 2)
    picked = jax.vmap(lambda one_key: jax.random.permutation(one_key, NODE_DEV - 1)[:2 * FACE - 1])(jax.random.split(key_pick, devices))
    with_last = jnp.concatenate([picked.astype(jnp.int32), jnp.full((devices, 1), NODE_DEV - 1, jnp.int32)], axis=1)
    mixing = jax.vmap(lambda one_key: jax.random.permutation(one_key, 2 * FACE))(jax.random.split(key_mix, devices))
    mixed = jnp.take_along_axis(with_last, mixing.astype(jnp.int32), axis=1)
    return mixed.reshape(devices, 2, FACE).transpose(1, 0, 2).reshape(2, devices * FACE).astype(jnp.int32)


def draw_stiffness(key, part):
    key_size, key_sign, key_diag = jax.random.split(jax.random.fold_in(key, 404), 3)
    magnitude = jax.random.uniform(key_size, (2, DOFS, DOFS), jnp.float32, 0.5, 1.0)
    size_part = 0.5 * (magnitude + jnp.transpose(magnitude, (0, 2, 1)))
    sign_raw = jax.random.normal(key_sign, (2, DOFS), jnp.float32)
    sign_vector = jnp.where(sign_raw >= 0.0, 1.0, -1.0)
    block_sign = jnp.array([1.0, -1.0], jnp.float32)[:, None, None]
    sign_part = block_sign * sign_vector[:, :, None] * sign_vector[:, None, :]
    identity = jnp.eye(DOFS, dtype=jnp.float32)
    lift = jax.random.uniform(key_diag, (2, DOFS), jnp.float32, 0.0, 40.0)
    diag_part = (DOFS + lift)[:, :, None] * identity
    return ((size_part * sign_part * (1.0 - identity) + diag_part) / 232.0).astype(jnp.float32)


def shard_levels(stream_key, dims, cuts, smallest, top_value):
    def one(axis_at, blocks):
        heights = jax.random.uniform(jax.random.fold_in(jax.random.fold_in(stream_key, 6), axis_at), (blocks,), jnp.float32, smallest / len(cuts), top_value / len(cuts))
        return jnp.repeat(jnp.exp(heights), dims[axis_at] // blocks).reshape((-1,) + (1,) * (len(dims) - axis_at - 1))

    gain = one(*cuts[0])
    for cut in cuts[1:]:
        gain = gain * one(*cut)
    return gain


def scatter_about(key, extent, scale, limit, cuts=(), held_as=jnp.bfloat16):
    level = shard_levels(key, extent, cuts, -0.22, 0.18) if cuts else 1.0
    values = jax.random.normal(key, extent, jnp.float32) * scale * level
    return jnp.minimum(jnp.maximum(values, -limit), limit).astype(held_as)


def setup_inputs(seed: int = 0) -> dict:
    splits = jax.random.split(jax.random.key(seed), 8)
    start_field = scatter_about(splits[0], (3, NODES), 1.0, 6.0, ((1, 32),), jnp.float32)
    element_loads = scatter_about(splits[1], (DOFS, ELEMENTS), 1.0, 6.0, ((1, 32),), jnp.float32)
    element_coefs = jnp.clip(jnp.exp(math.log(5.0) - 3.218876 * jax.random.uniform(splits[2], (2, ELEMENTS), jnp.float32) ** shard_levels(splits[2], (2, ELEMENTS), ((1, 32),), -0.2, 0.2)), 0.2, 5.0)
    element_nodes = draw_element_nodes(jax.random.fold_in(splits[7], 71), 0)
    move_list = draw_move_list(jax.random.fold_in(splits[7], 71), 0)
    face_nodes = draw_face_nodes(jax.random.fold_in(splits[7], 71), 0)
    stiffness = draw_stiffness(jax.random.fold_in(splits[7], 71), 0)
    return {"start_field": start_field, "element_loads": element_loads, "element_coefs": element_coefs, "element_nodes": element_nodes, "move_list": move_list, "face_nodes": face_nodes, "stiffness": stiffness}


center = 1.125
half_width = 0.875


def reference(start_field, element_loads, element_coefs, element_nodes, move_list, face_nodes, stiffness):
    devices = ELEMENTS // ELEM_DEV
    per_element = element_nodes.shape[0]
    dof_count = element_loads.shape[0]
    components = dof_count // per_element
    destination = move_list[0] * ELEM_DEV + move_list[1]
    moved_loads = jnp.zeros_like(element_loads).at[:, destination].set(element_loads)
    moved_coefs = jnp.zeros_like(element_coefs).at[:, destination].set(element_coefs)
    owner_device = (jnp.arange(ELEMENTS, dtype=jnp.int32) // ELEM_DEV)[None, :]
    face_lists = face_nodes.reshape(2, devices, FACE)
    slot_back = jnp.clip(element_nodes - NODE_DEV, 0, FACE - 1)
    slot_ahead = jnp.clip(element_nodes - NODE_DEV - FACE, 0, FACE - 1)
    prev_device = jnp.clip(owner_device - 1, 0, devices - 1)
    next_device = jnp.clip(owner_device + 1, 0, devices - 1)
    from_prev = prev_device * NODE_DEV + face_lists[1][prev_device, slot_back]
    from_next = next_device * NODE_DEV + face_lists[0][next_device, slot_ahead]
    global_nodes = jnp.where(element_nodes < NODE_DEV, owner_device * NODE_DEV + element_nodes,
                             jnp.where(element_nodes < NODE_DEV + FACE, from_prev, from_next))
    flat_nodes = global_nodes.reshape(-1).astype(jnp.int32)

    def assemble(values):
        channels = values.shape[0] // per_element
        return jnp.zeros((channels, NODES), jnp.float32).at[:, flat_nodes].add(values.reshape(channels, -1))

    def operate(field):
        gathered = field[:, flat_nodes].reshape(dof_count, ELEMENTS)
        part_first = jnp.dot(stiffness[0], gathered, precision=lax.Precision.HIGHEST, preferred_element_type=jnp.float32)
        part_second = jnp.dot(stiffness[1], gathered, precision=lax.Precision.HIGHEST, preferred_element_type=jnp.float32)
        return assemble(part_first * moved_coefs[0] + part_second * moved_coefs[1])

    diagonals = jnp.diagonal(stiffness, axis1=1, axis2=2)
    element_diag = diagonals[0][:, None] * moved_coefs[0] + diagonals[1][:, None] * moved_coefs[1]
    right_side = assemble(moved_loads)
    diagonal = assemble(element_diag)
    field = start_field
    scaled_center = center / half_width
    for sweep_index in range(SWEEPS):
        residual = right_side - operate(field)
        update = residual / (center * diagonal)
        ratio = 1.0 / scaled_center
        for degree_step in range(DEGREE):
            field = field + update
            if degree_step + 1 < DEGREE:
                residual = residual - operate(update)
                ratio_next = 1.0 / (2.0 * scaled_center - ratio)
                update = ratio_next * ratio * update + (2.0 * ratio_next / half_width) * residual / diagonal
                ratio = ratio_next
    return field, moved_loads, moved_coefs
```

```python
import functools

import jax
import jax.numpy as jnp
from jax import lax
from jax.experimental import pallas as pl
from jax.experimental.pallas import tpu as pltpu
from jax.sharding import PartitionSpec as P

NEAR_CAP = 16
DEGREE = 4
SWEEPS = 2
LOW = 32
GROUP = 8
LANES = 128

center = 1.125
half_width = 0.875

f32 = jnp.float32
bf16 = jnp.bfloat16
i32 = jnp.int32
HIGHEST = lax.Precision.HIGHEST


def chebyshev_weights():
    weights = []
    scaled_center = center / half_width
    for sweep_index in range(SWEEPS):
        if sweep_index:
            weights.append((0.0, 1.0 / center))
        ratio = 1.0 / scaled_center
        for _ in range(DEGREE - 1):
            ratio_next = 1.0 / (2.0 * scaled_center - ratio)
            weights.append((ratio_next * ratio, 2.0 * ratio_next / half_width))
            ratio = ratio_next
    return weights


def split(x):
    high = x.astype(bf16)
    return high, (x - high.astype(f32)).astype(bf16)


def dot(a, b):
    return jnp.dot(a, b, preferred_element_type=f32)


def dot_nt(a, b, precision=None):
    return lax.dot_general(
        a, b, (((1,), (1,)), ((), ())), precision=precision, preferred_element_type=f32
    )


def pick_low(found, low_row, components):
    mask = lax.broadcasted_iota(i32, (LOW, low_row.shape[1]), 0) == low_row
    half = components * LOW
    both = found[:half] + found[half:]
    return [
        jnp.sum(jnp.where(mask, both[c * LOW : (c + 1) * LOW], 0.0), axis=0, keepdims=True)
        for c in range(components)
    ]


def spread_low(rows, low_row):
    mask = lax.broadcasted_iota(i32, (LOW, low_row.shape[1]), 0) == low_row
    tall = []
    for part in range(2):
        for row in rows:
            high = row.astype(bf16).astype(f32)
            piece = high if part == 0 else row - high
            tall.append(jnp.where(mask, piece, 0.0).astype(bf16))
    return jnp.concatenate(tall, axis=0)


def one_hot_rows(row, count):
    hit = lax.broadcasted_iota(i32, (count, row.shape[1]), 0) == row
    return jnp.where(hit, 1.0, 0.0).astype(bf16)


def kernel(
    devices, subs, owned, face,
    start_ref, loads_ref, coefs_ref, nodes_ref, moves_ref, face_smem, face_ref, stiff_ref,
    out_ref, moved_loads_ref, moved_coefs_ref,
    onehot, onehot_t, column_t, high_ref, low_ref, stiff_high, stiff_low, x_ref, y_ref,
    update_ref, residual_ref, inverse_ref, delta_ref, total_ref,
    far_out, far_in, near_out, near_in, records, edge_out, edge_in,
    far_send, far_recv, near_send, near_recv, edge_send, edge_recv,
):
    per_element, slots = nodes_ref.shape
    dofs = loads_ref.shape[0]
    components = dofs // per_element
    height = components * LOW
    columns = owned // LOW
    width = face // LOW
    table = onehot.shape[1]
    groups = per_element // GROUP
    me = lax.axis_index("seg") * subs + lax.axis_index("sub")
    has_prev = me > 0
    has_next = me < devices - 1

    def coords(p):
        return {"seg": lax.div(p, subs), "sub": lax.rem(p, subs)}

    before = coords(jnp.maximum(me - 1, 0))
    after = coords(jnp.minimum(me + 1, devices - 1))

    far_in[me] = jnp.zeros((1, slots), f32)
    near_in[...] = jnp.zeros_like(near_in)
    barrier = pltpu.get_barrier_semaphore()

    def greet(d, _):
        pl.semaphore_signal(
            barrier, inc=1, device_id=coords(lax.rem(me + d, devices)),
            device_id_type=pl.DeviceIdType.MESH,
        )
        return 0

    lax.fori_loop(1, devices, greet, 0)

    def edge_copy(way, t):
        return pltpu.make_async_remote_copy(
            src_ref=edge_out.at[t], dst_ref=edge_in.at[way, t],
            send_sem=edge_send.at[way, t], recv_sem=edge_recv.at[way, t],
            device_id=after if way == 0 else before, device_id_type=pl.DeviceIdType.MESH,
        )

    def near_copy(way):
        return pltpu.make_async_remote_copy(
            src_ref=near_out.at[way], dst_ref=near_in.at[way],
            send_sem=near_send.at[way], recv_sem=near_recv.at[way],
            device_id=after if way == 0 else before, device_id_type=pl.DeviceIdType.MESH,
        )

    def both_ways(copies):
        @pl.when(has_next)
        def _():
            copies[0].start()

        @pl.when(has_prev)
        def _():
            copies[1].start()

    def finish(copies):
        @pl.when(has_prev)
        def _():
            copies[0].wait_recv()
            copies[1].wait_send()

        @pl.when(has_next)
        def _():
            copies[1].wait_recv()
            copies[0].wait_send()

    def send_edge(part, t):
        edge_out[t] = part[:, table - LANES :]
        both_ways([edge_copy(0, t), edge_copy(1, t)])

    lane = lax.broadcasted_iota(i32, (height, LANES), 1) - (columns - (table - LANES))

    def receive_edge(part, t):
        finish([edge_copy(0, t), edge_copy(1, t)])
        from_prev = pltpu.roll(edge_in[0, t], 2 * width, 1)
        from_next = pltpu.roll(edge_in[1, t], LANES - 2 * width, 1)
        take_prev = (lane >= 2 * width) & (lane < 4 * width) & has_prev
        take_next = (lane >= 0) & (lane < 2 * width) & has_next
        tail = part[:, table - LANES :]
        tail = tail + jnp.where(take_prev, from_prev, jnp.where(take_next, from_next, 0.0))
        return jnp.concatenate([part[:, : table - LANES], tail], axis=1)

    face_row = face_ref[...]
    face_low = ((face_row.astype(f32) + 0.5) * (1.0 / columns)).astype(i32)
    face_old = one_hot_rows(face_row - face_low * columns, table)
    place = lax.broadcasted_iota(i32, face_row.shape, 1)
    face_new_low = place & (LOW - 1)
    face_new = one_hot_rows(lax.div(place, LOW) + columns + width, table)

    start = jnp.concatenate(
        [start_ref[...], jnp.zeros((height, table - columns), f32)], axis=1
    )
    face_values = pick_low(dot(jnp.concatenate(split(start), 0), face_old), face_low, components)
    lifted = dot_nt(spread_low(face_values, face_new_low), face_new)
    field = start + lifted[:height] + lifted[height:]

    dest = moves_ref[0:1, :]
    new_slot = moves_ref[1:2, :]
    spot = moves_ref[2:3, :]
    staying = dest == me
    row_of = jnp.where(
        dest == me + 1, devices + spot,
        jnp.where(dest == me - 1, devices + NEAR_CAP + spot, dest),
    )
    row_of = jnp.where(staying, -1, row_of)
    record = jnp.concatenate(
        [
            loads_ref[...], coefs_ref[...], (new_slot + 1).astype(f32),
            jnp.zeros((slots - dofs - 3, slots), f32),
        ],
        axis=0,
    )
    rows = devices + 2 * NEAR_CAP
    chosen = lax.broadcasted_iota(i32, (rows, slots), 0) == row_of
    packed = dot_nt(jnp.where(chosen, 1.0, 0.0), record, HIGHEST)
    for p in range(devices):
        far_out[p] = packed[p : p + 1]
    near_out[0] = packed[devices : devices + NEAR_CAP]
    near_out[1] = packed[devices + NEAR_CAP :]

    def far_copy(p, row):
        return pltpu.make_async_remote_copy(
            src_ref=far_out.at[p], dst_ref=far_in.at[row],
            send_sem=far_send.at[p], recv_sem=far_recv.at[row],
            device_id=coords(p), device_id_type=pl.DeviceIdType.MESH,
        )

    pl.semaphore_wait(barrier, devices - 1)
    send_edge(field, 0)
    both_ways([near_copy(0), near_copy(1)])

    def far_start(d, _):
        far_copy(lax.rem(me + d, devices), me).start()
        return 0

    lax.fori_loop(1, devices, far_start, 0)

    nodes = nodes_ref[...]
    extra = jnp.where(
        nodes < owned, -1, jnp.where(nodes < owned + face, nodes - owned + 3 * face, nodes - owned - face)
    )

    def relabel(s, extra):
        extra = jnp.where(nodes == face_smem[1, s], face + s, extra)
        return jnp.where(nodes == face_smem[0, s], 2 * face + s, extra)

    extra = lax.fori_loop(0, face, relabel, extra, unroll=4)
    own_low = ((nodes.astype(f32) + 0.5) * (1.0 / columns)).astype(i32)
    low = jnp.where(extra >= 0, extra & (LOW - 1), own_low)
    high = jnp.where(extra >= 0, columns + lax.div(extra, LOW), nodes - own_low * columns)
    high_ref[...] = high
    low_ref[...] = low
    high_t = jnp.transpose(high.astype(f32)).astype(i32)
    for g in range(groups):
        column_t[g] = high_t[:, g * GROUP : (g + 1) * GROUP]

    def build(g, _):
        own = column_t[g]
        rows8 = high_ref[pl.ds(pl.multiple_of(g * GROUP, GROUP), GROUP), :]
        for j in range(GROUP):
            n = g * GROUP + j
            onehot[n] = one_hot_rows(rows8[j : j + 1], table)
            hit = lax.broadcasted_iota(i32, (slots, table), 1) == own[:, j : j + 1]
            onehot_t[pl.ds(pl.multiple_of(n * slots, slots), slots), :] = jnp.where(
                hit, 1.0, 0.0
            ).astype(bf16)
        return 0

    lax.fori_loop(0, groups, build, 0)

    stiff = stiff_ref[...]
    stiff_high[...] = stiff.astype(bf16)
    stiff_low[...] = (stiff - stiff_high[...].astype(f32)).astype(bf16)

    def gather(values):
        both = jnp.concatenate(split(values), axis=0)

        def step(g, _):
            low8 = low_ref[pl.ds(pl.multiple_of(g * GROUP, GROUP), GROUP), :]
            found = [[] for _ in range(components)]
            for j in range(GROUP):
                rows = pick_low(dot(both, onehot[g * GROUP + j]), low8[j : j + 1], components)
                for c in range(components):
                    found[c].append(rows[c])
            for c in range(components):
                at = pl.multiple_of(c * per_element + g * GROUP, GROUP)
                x_ref[pl.ds(at, GROUP), :] = jnp.concatenate(found[c], axis=0)
            return 0

        lax.fori_loop(0, groups, step, 0)

    def scatter(values):
        y_ref[...] = values
        total_ref[...] = jnp.zeros_like(total_ref)

        def step(g, _):
            low8 = low_ref[pl.ds(pl.multiple_of(g * GROUP, GROUP), GROUP), :]
            parts = [
                y_ref[pl.ds(pl.multiple_of(c * per_element + g * GROUP, GROUP), GROUP), :]
                for c in range(components)
            ]
            wide = jnp.concatenate(
                [
                    spread_low([part[j : j + 1] for part in parts], low8[j : j + 1])
                    for j in range(GROUP)
                ],
                axis=1,
            )
            at = pl.multiple_of(g * GROUP * slots, GROUP * slots)
            total_ref[...] += dot(wide, onehot_t[pl.ds(at, GROUP * slots), :])
            return 0

        lax.fori_loop(0, groups, step, 0)
        return total_ref[:height] + total_ref[height:]

    def products():
        x_high, x_low = split(x_ref[...])
        return dot(stiff_high[...], x_high) + (
            dot(stiff_low[...], x_high) + dot(stiff_high[...], x_low)
        )

    field = receive_edge(field, 0)
    gather(field)
    both = products()

    finish([near_copy(0), near_copy(1)])

    def far_finish(d, _):
        p = lax.rem(me + d, devices)
        far_copy(p, p).wait_recv()
        far_copy(p, p).wait_send()
        return 0

    lax.fori_loop(1, devices, far_finish, 0)
    records[...] = jnp.zeros_like(records)
    for p in range(devices):
        records[p : p + 1, :] = far_in[p]
    records[devices : devices + NEAR_CAP, :] = near_in[0]
    records[devices + NEAR_CAP : devices + 2 * NEAR_CAP, :] = near_in[1]
    got = records[...]
    slot_of = got[:, dofs + 2 : dofs + 3]
    aim = lax.broadcasted_iota(i32, (got.shape[0], slots), 1).astype(f32) + 1.0
    landing = jnp.where(aim == slot_of, 1.0, 0.0)
    arrived = jnp.dot(
        jnp.transpose(got), landing, precision=HIGHEST, preferred_element_type=f32
    )
    moved = jnp.where(staying, record, 0.0) + arrived
    loads = moved[:dofs]
    coefs = moved[dofs : dofs + 2]
    moved_loads_ref[...] = loads
    moved_coefs_ref[...] = coefs
    first, second = coefs[0:1], coefs[1:2]

    def element_values(both):
        return both[:dofs] * first + both[dofs:] * second

    on_diagonal = lax.broadcasted_iota(i32, (dofs, dofs), 0) == lax.broadcasted_iota(
        i32, (dofs, dofs), 1
    )
    diagonals = [
        jnp.sum(jnp.where(on_diagonal, stiff[k * dofs : (k + 1) * dofs], 0.0), axis=1, keepdims=True)
        for k in range(2)
    ]
    part = scatter(loads - element_values(both))
    send_edge(part, 1)
    diagonal = scatter(diagonals[0] * first + diagonals[1] * second)
    send_edge(diagonal, 2)
    residual = receive_edge(part, 1)
    diagonal = receive_edge(diagonal, 2)
    inverse = jnp.where(diagonal > 0.0, 1.0 / diagonal, 0.0)
    inverse_ref[...] = inverse
    residual_ref[...] = residual
    update_ref[...] = residual * inverse * (1.0 / center)
    delta_ref[...] = jnp.zeros_like(delta_ref)
    weights = chebyshev_weights()

    def sweep_step(i, _):
        update = update_ref[...]
        delta_ref[...] += update
        gather(update)
        part = scatter(element_values(products()))
        send_edge(part, 3 + i)
        residual = residual_ref[...] - receive_edge(part, 3 + i)
        residual_ref[...] = residual
        old, new = jnp.float32(0.0), jnp.float32(0.0)
        for k, (a, b) in enumerate(weights):
            old = jnp.where(i == k, a, old)
            new = jnp.where(i == k, b, new)
        update_ref[...] = old * update + new * (residual * inverse_ref[...])
        return 0

    lax.fori_loop(0, len(weights), sweep_step, 0)

    delta = delta_ref[...] + update_ref[...]
    face_values = pick_low(
        dot(jnp.concatenate(split(delta), 0), face_new), face_new_low, components
    )
    lowered = dot_nt(spread_low(face_values, face_low), face_old)
    result = start + delta + lowered[:height] + lowered[height:]
    out_ref[...] = result[:, :columns]


def local(
    devices, subs,
    start_field, element_loads, element_coefs, element_nodes, move_list, face_nodes, stiffness,
):
    dofs, slots = element_loads.shape
    per_element = element_nodes.shape[0]
    components = dofs // per_element
    owned = start_field.shape[1]
    face = face_nodes.shape[1]
    height = components * LOW
    columns = owned // LOW
    table = -(-(columns + 4 * (face // LOW)) // LANES) * LANES
    groups = per_element // GROUP
    rows = -(-(devices + 2 * NEAR_CAP) // LANES) * LANES
    edges = 2 + SWEEPS * DEGREE
    vmem = pl.BlockSpec(memory_space=pltpu.VMEM)
    smem = pl.BlockSpec(memory_space=pltpu.SMEM)
    wide = (height, table)
    smoothed, moved_loads, moved_coefs = pl.pallas_call(
        functools.partial(kernel, devices, subs, owned, face),
        out_shape=(
            jax.ShapeDtypeStruct((height, columns), f32),
            jax.ShapeDtypeStruct((dofs, slots), f32),
            jax.ShapeDtypeStruct((2, slots), f32),
        ),
        in_specs=[vmem] * 5 + [smem, vmem, vmem],
        out_specs=(vmem, vmem, vmem),
        scratch_shapes=[
            pltpu.VMEM((per_element, table, slots), bf16),
            pltpu.VMEM((per_element * slots, table), bf16),
            pltpu.VMEM((groups, slots, GROUP), i32),
            pltpu.VMEM((per_element, slots), i32),
            pltpu.VMEM((per_element, slots), i32),
            pltpu.VMEM((2 * dofs, dofs), bf16),
            pltpu.VMEM((2 * dofs, dofs), bf16),
            pltpu.VMEM((dofs, slots), f32),
            pltpu.VMEM((dofs, slots), f32),
            pltpu.VMEM(wide, f32),
            pltpu.VMEM(wide, f32),
            pltpu.VMEM(wide, f32),
            pltpu.VMEM(wide, f32),
            pltpu.VMEM((2 * height, table), f32),
            pltpu.VMEM((devices, 1, slots), f32),
            pltpu.VMEM((devices, 1, slots), f32),
            pltpu.VMEM((2, NEAR_CAP, slots), f32),
            pltpu.VMEM((2, NEAR_CAP, slots), f32),
            pltpu.VMEM((rows, slots), f32),
            pltpu.VMEM((edges, height, LANES), f32),
            pltpu.VMEM((2, edges, height, LANES), f32),
            pltpu.SemaphoreType.DMA((devices,)),
            pltpu.SemaphoreType.DMA((devices,)),
            pltpu.SemaphoreType.DMA((2,)),
            pltpu.SemaphoreType.DMA((2,)),
            pltpu.SemaphoreType.DMA((2, edges)),
            pltpu.SemaphoreType.DMA((2, edges)),
        ],
        compiler_params=pltpu.CompilerParams(
            collective_id=0, has_side_effects=True, vmem_limit_bytes=48 * 1024 * 1024
        ),
        name="migrate_and_smooth",
    )(
        start_field.reshape(height, columns),
        element_loads,
        element_coefs,
        element_nodes,
        move_list,
        face_nodes,
        jnp.concatenate([face_nodes[1], face_nodes[0]])[None, :],
        stiffness.reshape(2 * dofs, dofs),
    )
    return smoothed.reshape(components, owned), moved_loads, moved_coefs


def solution(mesh):
    devices = mesh.shape["seg"] * mesh.shape["sub"]
    return jax.shard_map(
        functools.partial(local, devices, mesh.shape["sub"]),
        mesh=mesh,
        in_specs=(
            P(None, ("seg", "sub")),
            P(None, ("seg", "sub")),
            P(None, ("seg", "sub")),
            P(None, ("seg", "sub")),
            P(None, ("seg", "sub")),
            P(None, ("seg", "sub")),
            P(),
        ),
        out_specs=(P(None, ("seg", "sub")), P(None, ("seg", "sub")), P(None, ("seg", "sub"))),
        check_vma=False,
    )
```

```python
import functools

import jax
import jax.numpy as jnp
from jax import lax
from jax.experimental import pallas as pl
from jax.experimental.pallas import tpu as pltpu
from jax.sharding import PartitionSpec as P

NEAR_CAP = 16
DEGREE = 4
SWEEPS = 2
COLUMNS = 256
TILE = 8
GROUP = 8
LANES = 128
UNROLL = 4

center = 1.125
half_width = 0.875

f32 = jnp.float32
bf16 = jnp.bfloat16
i32 = jnp.int32
HIGHEST = lax.Precision.HIGHEST


def chebyshev_weights():
    weights = []
    scaled_center = center / half_width
    for sweep_index in range(SWEEPS):
        if sweep_index:
            weights.append((0.0, 1.0 / center))
        ratio = 1.0 / scaled_center
        for _ in range(DEGREE - 1):
            ratio_next = 1.0 / (2.0 * scaled_center - ratio)
            weights.append((ratio_next * ratio, 2.0 * ratio_next / half_width))
            ratio = ratio_next
    return weights


def split(x):
    high = x.astype(bf16)
    return high, (x - high.astype(f32)).astype(bf16)


def dot(a, b):
    return jnp.dot(a, b, preferred_element_type=f32)


def dot_nt(a, b, precision=None):
    return lax.dot_general(
        a, b, (((1,), (1,)), ((), ())), precision=precision, preferred_element_type=f32
    )


def pick_low(found, low_row, components):
    half = found.shape[0] // 2
    depth = half // components
    mask = lax.broadcasted_iota(i32, (depth, low_row.shape[1]), 0) == low_row
    both = found[:half] + found[half:]
    return [
        jnp.sum(jnp.where(mask, both[c * depth : (c + 1) * depth], 0.0), axis=0, keepdims=True)
        for c in range(components)
    ]


def spread_low(rows, low_row, depth):
    mask = lax.broadcasted_iota(i32, (depth, low_row.shape[1]), 0) == low_row
    tall = []
    for part in range(2):
        for row in rows:
            high = row.astype(bf16).astype(f32)
            piece = high if part == 0 else row - high
            tall.append(jnp.where(mask, piece, 0.0).astype(bf16))
    return jnp.concatenate(tall, axis=0)


def one_hot_rows(row, count):
    hit = lax.broadcasted_iota(i32, (count, row.shape[1]), 0) == row
    return jnp.where(hit, 1.0, 0.0).astype(bf16)


def kernel(
    devices, subs,
    start_hbm, loads_hbm, coefs_ref, nodes_hbm, moves_ref, face_smem, face_ref, stiff_hbm,
    out_ref, moved_loads_ref, moved_coefs_ref,
    start_ref, loads_ref, nodes_ref, stiff_ref, arrive,
    onehot, onehot_t, column_t, low_ref, high_ref, stiff_high, stiff_low, x_ref, y_ref,
    start_table, update_ref, residual_ref, inverse_ref, delta_ref, total_ref,
    far_out, far_in, near_out, near_in, records, edge_out, edge_in,
    far_send, far_recv, near_send, near_recv, edge_send, edge_recv,
):
    per_element, slots = nodes_ref.shape
    dofs = loads_ref.shape[0]
    components = dofs // per_element
    owned = start_ref.shape[1]
    face = face_ref.shape[1]
    height = start_table.shape[0]
    depth = height // components
    own_rows = owned // COLUMNS
    edges = edge_out.shape[1]
    groups = per_element // GROUP
    me = lax.axis_index("seg") * subs + lax.axis_index("sub")
    has_prev = me > 0
    has_next = me < devices - 1

    incoming = [
        pltpu.make_async_copy(source, target, arrive.at[k])
        for k, (source, target) in enumerate(
            [(loads_hbm, loads_ref), (start_hbm, start_ref), (nodes_hbm, nodes_ref), (stiff_hbm, stiff_ref)]
        )
    ]
    for copy in incoming:
        copy.start()

    def coords(p):
        return {"seg": lax.div(p, subs), "sub": lax.rem(p, subs)}

    before = coords(jnp.maximum(me - 1, 0))
    after = coords(jnp.minimum(me + 1, devices - 1))

    far_in[me] = jnp.zeros((1, slots), f32)
    near_in[...] = jnp.zeros_like(near_in)
    barrier = pltpu.get_barrier_semaphore()

    def greet(d, _):
        pl.semaphore_signal(
            barrier, inc=1, device_id=coords(lax.rem(me + d, devices)),
            device_id_type=pl.DeviceIdType.MESH,
        )
        return 0

    lax.fori_loop(1, devices, greet, 0)

    def edge_copy(way, t):
        return pltpu.make_async_remote_copy(
            src_ref=edge_out.at[way, t], dst_ref=edge_in.at[way, t],
            send_sem=edge_send.at[way, t], recv_sem=edge_recv.at[way, t],
            device_id=after if way == 0 else before, device_id_type=pl.DeviceIdType.MESH,
        )

    def near_copy(way):
        return pltpu.make_async_remote_copy(
            src_ref=near_out.at[way], dst_ref=near_in.at[way],
            send_sem=near_send.at[way], recv_sem=near_recv.at[way],
            device_id=after if way == 0 else before, device_id_type=pl.DeviceIdType.MESH,
        )

    def both_ways(copies):
        @pl.when(has_next)
        def _():
            copies[0].start()

        @pl.when(has_prev)
        def _():
            copies[1].start()

    def receive(copies):
        @pl.when(has_prev)
        def _():
            copies[0].wait_recv()

        @pl.when(has_next)
        def _():
            copies[1].wait_recv()

    def sent(copies):
        @pl.when(has_next)
        def _():
            copies[0].wait_send()

        @pl.when(has_prev)
        def _():
            copies[1].wait_send()

    top = own_rows % TILE
    tile_at = own_rows - top
    sublane = lax.broadcasted_iota(i32, (TILE, LANES), 0)

    def send_edge(part, t):
        for c in range(components):
            at = c * depth + tile_at
            left, right = part[at : at + TILE, :LANES], part[at : at + TILE, LANES:]
            edge_out[0, t, c] = jnp.where(sublane == top + 2, pltpu.roll(right, 2, 0), left)
            edge_out[1, t, c] = jnp.where(sublane == top, pltpu.roll(left, TILE - 2, 0), right)
        both_ways([edge_copy(0, t), edge_copy(1, t)])

    first_row, middle_row, last_row = (sublane == top + k for k in range(3))

    def receive_edge(part, t):
        receive([edge_copy(0, t), edge_copy(1, t)])
        pieces = []
        for c in range(components):
            at = c * depth + tile_at
            left, right = part[at : at + TILE, :LANES], part[at : at + TILE, LANES:]
            prev, next_ = edge_in[0, t, c], edge_in[1, t, c]
            shifted = pltpu.roll(next_, TILE - 1, 0)
            left = left + jnp.where(
                last_row & has_prev, prev, jnp.where((first_row | middle_row) & has_next, shifted, 0.0)
            )
            shifted = pltpu.roll(prev, 1, 0)
            right = right + jnp.where(
                first_row & has_next, next_, jnp.where((middle_row | last_row) & has_prev, shifted, 0.0)
            )
            pieces += [
                part[c * depth : at], jnp.concatenate([left, right], axis=1),
                part[at + TILE : (c + 1) * depth],
            ]
        return jnp.concatenate([piece for piece in pieces if piece.shape[0]], axis=0)

    lists = []
    for k in range(2):
        old = face_ref[1 - k : 2 - k, :]
        new = owned + (1 + k) * face + lax.broadcasted_iota(i32, (1, face), 1)
        lists.append(
            [(node >> 8, one_hot_rows(node & (COLUMNS - 1), COLUMNS)) for node in (old, new)]
        )

    def move_faces(values, source, target):
        both = jnp.concatenate(split(values), axis=0)
        total = 0.0
        for places in lists:
            low, hot = places[source]
            rows = pick_low(dot(both, hot), low, components)
            low, hot = places[target]
            total = total + dot_nt(spread_low(rows, low, depth), hot)
        return total[:height] + total[height:]

    incoming[0].wait()
    incoming[1].wait()
    start_table[...] = jnp.zeros_like(start_table)
    for r in range(own_rows):
        for c in range(components):
            start_table[c * depth + r : c * depth + r + 1, :] = start_ref[
                c : c + 1, r * COLUMNS : (r + 1) * COLUMNS
            ]
    start = start_table[...]
    field = start + move_faces(start, 0, 1)

    dest = moves_ref[0:1, :]
    new_slot = moves_ref[1:2, :]
    spot = moves_ref[2:3, :]
    staying = dest == me
    row_of = jnp.where(
        dest == me + 1, devices + spot,
        jnp.where(dest == me - 1, devices + NEAR_CAP + spot, dest),
    )
    row_of = jnp.where(staying, -1, row_of)
    record = jnp.concatenate(
        [
            loads_ref[...], coefs_ref[...], (new_slot + 1).astype(f32),
            jnp.zeros((slots - dofs - 3, slots), f32),
        ],
        axis=0,
    )
    rows = devices + 2 * NEAR_CAP
    chosen = lax.broadcasted_iota(i32, (rows, slots), 0) == row_of
    packed = dot_nt(jnp.where(chosen, 1.0, 0.0), record, HIGHEST)
    for p in range(devices):
        far_out[p] = packed[p : p + 1]
    near_out[0] = packed[devices : devices + NEAR_CAP]
    near_out[1] = packed[devices + NEAR_CAP :]

    def far_copy(p, row):
        return pltpu.make_async_remote_copy(
            src_ref=far_out.at[p], dst_ref=far_in.at[row],
            send_sem=far_send.at[p], recv_sem=far_recv.at[row],
            device_id=coords(p), device_id_type=pl.DeviceIdType.MESH,
        )

    pl.semaphore_wait(barrier, devices - 1)
    send_edge(field, 0)
    both_ways([near_copy(0), near_copy(1)])

    def far_start(d, _):
        far_copy(lax.rem(me + d, devices), me).start()
        return 0

    lax.fori_loop(1, devices, far_start, 0)

    incoming[2].wait()
    nodes = nodes_ref[...]
    place = jnp.where(
        nodes < owned, nodes, jnp.where(nodes < owned + face, nodes + 3 * face, nodes - face)
    )

    def relabel(s, place):
        place = jnp.where(nodes == face_smem[1, s], owned + face + s, place)
        return jnp.where(nodes == face_smem[0, s], owned + 2 * face + s, place)

    place = lax.fori_loop(0, face, relabel, place, unroll=8)
    low_ref[...] = place >> 8
    column = place & (COLUMNS - 1)
    high_ref[...] = column
    column_rows = jnp.transpose(column.astype(f32)).astype(i32)
    for g in range(groups):
        column_t[g] = column_rows[:, g * GROUP : (g + 1) * GROUP]

    def build(g, _):
        own = column_t[g]
        rows8 = high_ref[pl.ds(pl.multiple_of(g * GROUP, GROUP), GROUP), :]
        for j in range(GROUP):
            n = g * GROUP + j
            onehot[n] = one_hot_rows(rows8[j : j + 1], COLUMNS)
            hit = lax.broadcasted_iota(i32, (slots, COLUMNS), 1) == own[:, j : j + 1]
            onehot_t[pl.ds(pl.multiple_of(n * slots, slots), slots), :] = jnp.where(
                hit, 1.0, 0.0
            ).astype(bf16)
        return 0

    lax.fori_loop(0, groups, build, 0)

    incoming[3].wait()
    stiff = stiff_ref[...]
    stiff_high[...] = stiff.astype(bf16)
    stiff_low[...] = (stiff - stiff_high[...].astype(f32)).astype(bf16)

    def gather(values):
        both = jnp.concatenate(split(values), axis=0)

        def step(g, _):
            low8 = low_ref[pl.ds(pl.multiple_of(g * GROUP, GROUP), GROUP), :]
            found = [[] for _ in range(components)]
            for j in range(GROUP):
                rows = pick_low(dot(both, onehot[g * GROUP + j]), low8[j : j + 1], components)
                for c in range(components):
                    found[c].append(rows[c])
            for c in range(components):
                at = pl.multiple_of(c * per_element + g * GROUP, GROUP)
                x_ref[pl.ds(at, GROUP), :] = jnp.concatenate(found[c], axis=0)
            return 0

        lax.fori_loop(0, groups, step, 0, unroll=UNROLL)

    def scatter(values):
        y_ref[...] = values
        total_ref[...] = jnp.zeros_like(total_ref)

        def step(g, _):
            low8 = low_ref[pl.ds(pl.multiple_of(g * GROUP, GROUP), GROUP), :]
            parts = [
                y_ref[pl.ds(pl.multiple_of(c * per_element + g * GROUP, GROUP), GROUP), :]
                for c in range(components)
            ]
            wide = jnp.concatenate(
                [
                    spread_low([part[j : j + 1] for part in parts], low8[j : j + 1], depth)
                    for j in range(GROUP)
                ],
                axis=1,
            )
            at = pl.multiple_of(g * GROUP * slots, GROUP * slots)
            total_ref[...] += dot(wide, onehot_t[pl.ds(at, GROUP * slots), :])
            return 0

        lax.fori_loop(0, groups, step, 0, unroll=UNROLL)
        return total_ref[:height] + total_ref[height:]

    def products():
        x_high, x_low = split(x_ref[...])
        return dot(stiff_high[...], x_high) + (
            dot(stiff_low[...], x_high) + dot(stiff_high[...], x_low)
        )

    field = receive_edge(field, 0)
    gather(field)
    both = products()

    receive([near_copy(0), near_copy(1)])

    def far_finish(d, _):
        p = lax.rem(me + d, devices)
        far_copy(p, p).wait_recv()
        return 0

    lax.fori_loop(1, devices, far_finish, 0)
    records[...] = jnp.zeros_like(records)
    for p in range(devices):
        records[p : p + 1, :] = far_in[p]
    records[devices : devices + NEAR_CAP, :] = near_in[0]
    records[devices + NEAR_CAP : devices + 2 * NEAR_CAP, :] = near_in[1]
    got = records[...]
    slot_of = got[:, dofs + 2 : dofs + 3]
    aim = lax.broadcasted_iota(i32, (got.shape[0], slots), 1).astype(f32) + 1.0
    landing = jnp.where(aim == slot_of, 1.0, 0.0)
    arrived = jnp.dot(
        jnp.transpose(got), landing, precision=HIGHEST, preferred_element_type=f32
    )
    moved = jnp.where(staying, record, 0.0) + arrived
    loads = moved[:dofs]
    coefs = moved[dofs : dofs + 2]
    moved_loads_ref[...] = loads
    moved_coefs_ref[...] = coefs
    first, second = coefs[0:1], coefs[1:2]

    def element_values(both):
        return both[:dofs] * first + both[dofs:] * second

    on_diagonal = lax.broadcasted_iota(i32, (dofs, dofs), 0) == lax.broadcasted_iota(
        i32, (dofs, dofs), 1
    )
    diagonals = [
        jnp.sum(jnp.where(on_diagonal, stiff[k * dofs : (k + 1) * dofs], 0.0), axis=1, keepdims=True)
        for k in range(2)
    ]
    part = scatter(loads - element_values(both))
    send_edge(part, 1)
    diagonal = scatter(diagonals[0] * first + diagonals[1] * second)
    send_edge(diagonal, 2)
    residual = receive_edge(part, 1)
    diagonal = receive_edge(diagonal, 2)
    inverse = jnp.where(diagonal > 0.0, 1.0 / diagonal, 0.0)
    inverse_ref[...] = inverse
    residual_ref[...] = residual
    update_ref[...] = residual * inverse * (1.0 / center)
    delta_ref[...] = jnp.zeros_like(delta_ref)
    weights = chebyshev_weights()

    def sweep_step(i, _):
        update = update_ref[...]
        delta_ref[...] += update
        gather(update)
        part = scatter(element_values(products()))
        send_edge(part, 3 + i)
        residual = residual_ref[...] - receive_edge(part, 3 + i)
        residual_ref[...] = residual
        old, new = jnp.float32(0.0), jnp.float32(0.0)
        for k, (a, b) in enumerate(weights):
            old = jnp.where(i == k, a, old)
            new = jnp.where(i == k, b, new)
        update_ref[...] = old * update + new * (residual * inverse_ref[...])
        return 0

    lax.fori_loop(0, len(weights), sweep_step, 0)

    delta = delta_ref[...] + update_ref[...]
    result = start_table[...] + delta + move_faces(delta, 1, 0)
    for r in range(own_rows):
        for c in range(components):
            out_ref[c : c + 1, r * COLUMNS : (r + 1) * COLUMNS] = result[
                c * depth + r : c * depth + r + 1
            ]

    sent([near_copy(0), near_copy(1)])

    def far_sent(d, _):
        far_copy(lax.rem(me + d, devices), me).wait_send()
        return 0

    lax.fori_loop(1, devices, far_sent, 0)

    def edge_sent(t, _):
        sent([edge_copy(0, t), edge_copy(1, t)])
        return 0

    lax.fori_loop(0, edges, edge_sent, 0)


def local(
    devices, subs,
    start_field, element_loads, element_coefs, element_nodes, move_list, face_nodes, stiffness,
):
    dofs, slots = element_loads.shape
    per_element = element_nodes.shape[0]
    components = dofs // per_element
    owned = start_field.shape[1]
    face = face_nodes.shape[1]
    extra_rows = 4 * face // COLUMNS
    own_rows = owned // COLUMNS
    assert owned % COLUMNS == 0 and 4 * face == 3 * COLUMNS and own_rows % TILE + 3 <= TILE
    depth = -(-(own_rows + extra_rows) // TILE) * TILE
    table = (components * depth, COLUMNS)
    groups = per_element // GROUP
    rows = -(-(devices + 2 * NEAR_CAP) // LANES) * LANES
    edges = 2 + SWEEPS * DEGREE
    vmem = pl.BlockSpec(memory_space=pltpu.VMEM)
    smem = pl.BlockSpec(memory_space=pltpu.SMEM)
    anywhere = pl.BlockSpec(memory_space=pl.ANY)
    return pl.pallas_call(
        functools.partial(kernel, devices, subs),
        out_shape=(
            jax.ShapeDtypeStruct(start_field.shape, f32),
            jax.ShapeDtypeStruct((dofs, slots), f32),
            jax.ShapeDtypeStruct((2, slots), f32),
        ),
        in_specs=[anywhere, anywhere, vmem, anywhere, vmem, smem, vmem, anywhere],
        out_specs=(vmem, vmem, vmem),
        scratch_shapes=[
            pltpu.VMEM(start_field.shape, f32),
            pltpu.VMEM((dofs, slots), f32),
            pltpu.VMEM((per_element, slots), i32),
            pltpu.VMEM((2 * dofs, dofs), f32),
            pltpu.SemaphoreType.DMA((4,)),
            pltpu.VMEM((per_element, COLUMNS, slots), bf16),
            pltpu.VMEM((per_element * slots, COLUMNS), bf16),
            pltpu.VMEM((groups, slots, GROUP), i32),
            pltpu.VMEM((per_element, slots), i32),
            pltpu.VMEM((per_element, slots), i32),
            pltpu.VMEM((2 * dofs, dofs), bf16),
            pltpu.VMEM((2 * dofs, dofs), bf16),
            pltpu.VMEM((dofs, slots), f32),
            pltpu.VMEM((dofs, slots), f32),
            pltpu.VMEM(table, f32),
            pltpu.VMEM(table, f32),
            pltpu.VMEM(table, f32),
            pltpu.VMEM(table, f32),
            pltpu.VMEM(table, f32),
            pltpu.VMEM((2 * table[0], COLUMNS), f32),
            pltpu.VMEM((devices, 1, slots), f32),
            pltpu.VMEM((devices, 1, slots), f32),
            pltpu.VMEM((2, NEAR_CAP, slots), f32),
            pltpu.VMEM((2, NEAR_CAP, slots), f32),
            pltpu.VMEM((rows, slots), f32),
            pltpu.VMEM((2, edges, components, TILE, LANES), f32),
            pltpu.VMEM((2, edges, components, TILE, LANES), f32),
            pltpu.SemaphoreType.DMA((devices,)),
            pltpu.SemaphoreType.DMA((devices,)),
            pltpu.SemaphoreType.DMA((2,)),
            pltpu.SemaphoreType.DMA((2,)),
            pltpu.SemaphoreType.DMA((2, edges)),
            pltpu.SemaphoreType.DMA((2, edges)),
        ],
        compiler_params=pltpu.CompilerParams(
            collective_id=0, has_side_effects=True, vmem_limit_bytes=56 * 1024 * 1024
        ),
        name="migrate_and_smooth",
    )(
        start_field,
        element_loads,
        element_coefs,
        element_nodes,
        move_list,
        face_nodes,
        face_nodes,
        stiffness.reshape(2 * dofs, dofs),
    )


def solution(mesh):
    devices = mesh.shape["seg"] * mesh.shape["sub"]
    return jax.shard_map(
        functools.partial(local, devices, mesh.shape["sub"]),
        mesh=mesh,
        in_specs=(
            P(None, ("seg", "sub")),
            P(None, ("seg", "sub")),
            P(None, ("seg", "sub")),
            P(None, ("seg", "sub")),
            P(None, ("seg", "sub")),
            P(None, ("seg", "sub")),
            P(),
        ),
        out_specs=(P(None, ("seg", "sub")), P(None, ("seg", "sub")), P(None, ("seg", "sub"))),
        check_vma=False,
    )
```

```python
import functools

import jax
import jax.numpy as jnp
from jax import lax
from jax.experimental import pallas as pl
from jax.experimental.pallas import tpu as pltpu
from jax.sharding import PartitionSpec as P

NEAR_CAP = 16
DEGREE = 4
SWEEPS = 2
COLUMNS = 256
TILE = 8
GROUP = 8
LANES = 128
UNROLL = 4

center = 1.125
half_width = 0.875

f32 = jnp.float32
bf16 = jnp.bfloat16
i32 = jnp.int32
HIGHEST = lax.Precision.HIGHEST


def chebyshev_weights():
    weights = []
    scaled_center = center / half_width
    for _ in range(SWEEPS):
        weights.append((0.0, 1.0 / center))
        ratio = 1.0 / scaled_center
        for _ in range(DEGREE - 1):
            ratio_next = 1.0 / (2.0 * scaled_center - ratio)
            weights.append((ratio_next * ratio, 2.0 * ratio_next / half_width))
            ratio = ratio_next
    return weights


def split(x):
    high = x.astype(bf16)
    return high, (x - high.astype(f32)).astype(bf16)


def dot(a, b):
    return jnp.dot(a, b, preferred_element_type=f32)


def dot_nt(a, b, precision=None):
    return lax.dot_general(
        a, b, (((1,), (1,)), ((), ())), precision=precision, preferred_element_type=f32
    )


def pick_low(found, low_row, components):
    half = found.shape[0] // 2
    depth = half // components
    mask = lax.broadcasted_iota(i32, (depth, low_row.shape[1]), 0) == low_row
    both = found[:half] + found[half:]
    return [
        jnp.sum(jnp.where(mask, both[c * depth : (c + 1) * depth], 0.0), axis=0, keepdims=True)
        for c in range(components)
    ]


def spread_low(rows, low_row, depth):
    mask = lax.broadcasted_iota(i32, (depth, low_row.shape[1]), 0) == low_row
    tall = []
    for part in range(2):
        for row in rows:
            high = row.astype(bf16).astype(f32)
            piece = high if part == 0 else row - high
            tall.append(jnp.where(mask, piece, 0.0).astype(bf16))
    return jnp.concatenate(tall, axis=0)


def one_hot_rows(row, count):
    numbers = lax.broadcasted_iota(i32, (count, row.shape[1]), 0).astype(f32).astype(bf16)
    hit = numbers == row.astype(f32).astype(bf16)
    return jnp.where(hit, jnp.ones_like(numbers), jnp.zeros_like(numbers))


def kernel(
    devices, subs,
    start_hbm, loads_hbm, coefs_ref, nodes_hbm, moves_ref, face_smem, face_ref, stiff_hbm,
    out_ref, moved_loads_ref, moved_coefs_ref,
    start_ref, loads_ref, nodes_ref, stiff_ref, arrive,
    onehot, onehot_t, column_t, low_ref, high_ref, extra_ref, stiff_high, stiff_low, x_ref, y_ref,
    start_table, update_ref, residual_ref, inverse_ref, delta_ref, part_ref, total_ref,
    far_out, far_in, near_out, near_in, records, edge_out, edge_in,
    far_send, far_recv, near_send, near_recv, edge_send, edge_recv,
):
    per_element, slots = nodes_ref.shape
    dofs = loads_ref.shape[0]
    components = dofs // per_element
    owned = start_ref.shape[1]
    face = face_ref.shape[1]
    height = start_table.shape[0]
    depth = height // components
    own_rows = owned // COLUMNS
    edges = edge_out.shape[1]
    groups = per_element // GROUP
    me = lax.axis_index("seg") * subs + lax.axis_index("sub")
    has_prev = me > 0
    has_next = me < devices - 1

    incoming = [
        pltpu.make_async_copy(source, target, arrive.at[k])
        for k, (source, target) in enumerate(
            [(loads_hbm, loads_ref), (start_hbm, start_ref), (nodes_hbm, nodes_ref), (stiff_hbm, stiff_ref)]
        )
    ]
    for copy in incoming:
        copy.start()

    def coords(p):
        return {"seg": lax.div(p, subs), "sub": lax.rem(p, subs)}

    before = coords(jnp.maximum(me - 1, 0))
    after = coords(jnp.minimum(me + 1, devices - 1))

    far_in[me] = jnp.zeros((1, slots), f32)
    near_in[...] = jnp.zeros_like(near_in)
    barrier = pltpu.get_barrier_semaphore()

    def greet(d, _):
        pl.semaphore_signal(
            barrier, inc=1, device_id=coords(lax.rem(me + d, devices)),
            device_id_type=pl.DeviceIdType.MESH,
        )
        return 0

    lax.fori_loop(1, devices, greet, 0)

    def edge_copy(way, t):
        return pltpu.make_async_remote_copy(
            src_ref=edge_out.at[way, t], dst_ref=edge_in.at[way, t],
            send_sem=edge_send.at[way, t], recv_sem=edge_recv.at[way, t],
            device_id=after if way == 0 else before, device_id_type=pl.DeviceIdType.MESH,
        )

    def near_copy(way):
        return pltpu.make_async_remote_copy(
            src_ref=near_out.at[way], dst_ref=near_in.at[way],
            send_sem=near_send.at[way], recv_sem=near_recv.at[way],
            device_id=after if way == 0 else before, device_id_type=pl.DeviceIdType.MESH,
        )

    def both_ways(copies):
        @pl.when(has_next)
        def _():
            copies[0].start()

        @pl.when(has_prev)
        def _():
            copies[1].start()

    def receive(copies):
        @pl.when(has_prev)
        def _():
            copies[0].wait_recv()

        @pl.when(has_next)
        def _():
            copies[1].wait_recv()

    def sent(copies):
        @pl.when(has_next)
        def _():
            copies[0].wait_send()

        @pl.when(has_prev)
        def _():
            copies[1].wait_send()

    top = own_rows % TILE
    tile_at = own_rows - top
    sublane = lax.broadcasted_iota(i32, (TILE, LANES), 0)

    def send_edge(part, t):
        for c in range(components):
            at = c * depth + tile_at
            left, right = part[at : at + TILE, :LANES], part[at : at + TILE, LANES:]
            edge_out[0, t, c] = jnp.where(sublane == top + 2, pltpu.roll(right, 2, 0), left)
            edge_out[1, t, c] = jnp.where(sublane == top, pltpu.roll(left, TILE - 2, 0), right)
        both_ways([edge_copy(0, t), edge_copy(1, t)])

    first_row, middle_row, last_row = (sublane == top + k for k in range(3))

    def receive_edge(part, t):
        receive([edge_copy(0, t), edge_copy(1, t)])
        pieces = []
        for c in range(components):
            at = c * depth + tile_at
            left, right = part[at : at + TILE, :LANES], part[at : at + TILE, LANES:]
            prev, next_ = edge_in[0, t, c], edge_in[1, t, c]
            shifted = pltpu.roll(next_, TILE - 1, 0)
            left = left + jnp.where(
                last_row & has_prev, prev, jnp.where((first_row | middle_row) & has_next, shifted, 0.0)
            )
            shifted = pltpu.roll(prev, 1, 0)
            right = right + jnp.where(
                first_row & has_next, next_, jnp.where((middle_row | last_row) & has_prev, shifted, 0.0)
            )
            pieces += [
                part[c * depth : at], jnp.concatenate([left, right], axis=1),
                part[at + TILE : (c + 1) * depth],
            ]
        return jnp.concatenate([piece for piece in pieces if piece.shape[0]], axis=0)

    lists = []
    for k in range(2):
        old = face_ref[1 - k : 2 - k, :]
        new = owned + (1 + k) * face + lax.broadcasted_iota(i32, (1, face), 1)
        lists.append(
            [(node >> 8, one_hot_rows(node & (COLUMNS - 1), COLUMNS)) for node in (old, new)]
        )

    def move_faces(values, source, target):
        both = jnp.concatenate(split(values), axis=0)
        total = 0.0
        for places in lists:
            low, hot = places[source]
            rows = pick_low(dot(both, hot), low, components)
            low, hot = places[target]
            total = total + dot_nt(spread_low(rows, low, depth), hot)
        return total[:height] + total[height:]

    incoming[0].wait()
    incoming[1].wait()
    start_table[...] = jnp.zeros_like(start_table)
    for r in range(own_rows):
        for c in range(components):
            start_table[c * depth + r : c * depth + r + 1, :] = start_ref[
                c : c + 1, r * COLUMNS : (r + 1) * COLUMNS
            ]
    start = start_table[...]
    field = start + move_faces(start, 0, 1)

    dest = moves_ref[0:1, :]
    new_slot = moves_ref[1:2, :]
    spot = moves_ref[2:3, :]
    staying = dest == me
    row_of = jnp.where(
        dest == me + 1, devices + spot,
        jnp.where(dest == me - 1, devices + NEAR_CAP + spot, dest),
    )
    row_of = jnp.where(staying, -1, row_of)
    record = jnp.concatenate(
        [
            loads_ref[...], coefs_ref[...], (new_slot + 1).astype(f32),
            jnp.zeros((slots - dofs - 3, slots), f32),
        ],
        axis=0,
    )
    rows = devices + 2 * NEAR_CAP
    chosen = lax.broadcasted_iota(i32, (rows, slots), 0) == row_of
    packed = dot_nt(jnp.where(chosen, 1.0, 0.0), record, HIGHEST)
    for p in range(devices):
        far_out[p] = packed[p : p + 1]
    near_out[0] = packed[devices : devices + NEAR_CAP]
    near_out[1] = packed[devices + NEAR_CAP :]

    def far_copy(p, row):
        return pltpu.make_async_remote_copy(
            src_ref=far_out.at[p], dst_ref=far_in.at[row],
            send_sem=far_send.at[p], recv_sem=far_recv.at[row],
            device_id=coords(p), device_id_type=pl.DeviceIdType.MESH,
        )

    pl.semaphore_wait(barrier, devices - 1)
    send_edge(field, 0)
    both_ways([near_copy(0), near_copy(1)])

    def far_start(d, _):
        far_copy(lax.rem(me + d, devices), me).start()
        return 0

    lax.fori_loop(1, devices, far_start, 0)

    incoming[2].wait()
    nodes = nodes_ref[...]
    place = jnp.where(
        nodes < owned, nodes, jnp.where(nodes < owned + face, nodes + 3 * face, nodes - face)
    )

    def relabel(s, place):
        place = jnp.where(nodes == face_smem[1, s], owned + face + s, place)
        return jnp.where(nodes == face_smem[0, s], owned + 2 * face + s, place)

    place = lax.fori_loop(0, face, relabel, place, unroll=8)
    low_ref[...] = place >> 8
    column = place & (COLUMNS - 1)
    high_ref[...] = column
    extra_ref[...] = place - owned
    column_rows = jnp.transpose(column.astype(f32))
    for g in range(groups):
        column_t[g] = column_rows[:, g * GROUP : (g + 1) * GROUP]

    def build(g, _):
        own = column_t[g].astype(bf16)
        numbers = lax.broadcasted_iota(i32, (slots, COLUMNS), 1).astype(f32).astype(bf16)
        rows8 = high_ref[pl.ds(pl.multiple_of(g * GROUP, GROUP), GROUP), :]
        for j in range(GROUP):
            n = g * GROUP + j
            onehot[n] = one_hot_rows(rows8[j : j + 1], COLUMNS)
            hit = numbers == own[:, j : j + 1]
            onehot_t[pl.ds(pl.multiple_of(n * slots, slots), slots), :] = jnp.where(
                hit, jnp.ones_like(numbers), jnp.zeros_like(numbers)
            )
        return 0

    lax.fori_loop(0, groups, build, 0)

    incoming[3].wait()
    stiff = stiff_ref[...]
    stiff_high[...] = stiff.astype(bf16)
    stiff_low[...] = (stiff - stiff_high[...].astype(f32)).astype(bf16)

    def gather(values):
        both = jnp.concatenate(split(values), axis=0)

        def step(g, _):
            low8 = low_ref[pl.ds(pl.multiple_of(g * GROUP, GROUP), GROUP), :]
            found = [[] for _ in range(components)]
            for j in range(GROUP):
                rows = pick_low(dot(both, onehot[g * GROUP + j]), low8[j : j + 1], components)
                for c in range(components):
                    found[c].append(rows[c])
            for c in range(components):
                at = pl.multiple_of(c * per_element + g * GROUP, GROUP)
                x_ref[pl.ds(at, GROUP), :] = jnp.concatenate(found[c], axis=0)
            return 0

        lax.fori_loop(0, groups, step, 0, unroll=UNROLL)

    def gather_interface(values):
        for side in range(slots // LANES):
            lanes = slice(side * LANES, (side + 1) * LANES)
            extra = extra_ref[:, lanes]
            lane_of = extra & (LANES - 1)
            piece_of = extra >> 7
            for c in range(components):
                rows = slice(c * per_element, (c + 1) * per_element)
                found = x_ref[rows, lanes]
                for piece in range(4 * face // LANES):
                    r = c * depth + own_rows + piece // 2
                    line = values[r : r + 1, (piece % 2) * LANES : (piece % 2 + 1) * LANES]
                    line = jnp.broadcast_to(line, (per_element, LANES))
                    taken = jnp.take_along_axis(line, lane_of, axis=1, mode="promise_in_bounds")
                    found = found + jnp.where(piece_of == piece, taken, 0.0)
                x_ref[rows, lanes] = found

    def scatter(values):
        y_ref[...] = values
        total_ref[...] = jnp.zeros_like(total_ref)

        def step(g, _):
            low8 = low_ref[pl.ds(pl.multiple_of(g * GROUP, GROUP), GROUP), :]
            parts = [
                y_ref[pl.ds(pl.multiple_of(c * per_element + g * GROUP, GROUP), GROUP), :]
                for c in range(components)
            ]
            wide = jnp.concatenate(
                [
                    spread_low([part[j : j + 1] for part in parts], low8[j : j + 1], depth)
                    for j in range(GROUP)
                ],
                axis=1,
            )
            at = pl.multiple_of(g * GROUP * slots, GROUP * slots)
            total_ref[...] += dot(wide, onehot_t[pl.ds(at, GROUP * slots), :])
            return 0

        lax.fori_loop(0, groups, step, 0, unroll=UNROLL)
        return total_ref[:height] + total_ref[height:]

    def products():
        x_high, x_low = split(x_ref[...])
        return dot(stiff_high[...], x_high) + (
            dot(stiff_low[...], x_high) + dot(stiff_high[...], x_low)
        )

    gather(start_table[...])
    gather_interface(receive_edge(field, 0))
    both = products()

    receive([near_copy(0), near_copy(1)])

    def far_finish(d, _):
        p = lax.rem(me + d, devices)
        far_copy(p, p).wait_recv()
        return 0

    lax.fori_loop(1, devices, far_finish, 0)
    records[...] = jnp.zeros_like(records)
    for p in range(devices):
        records[p : p + 1, :] = far_in[p]
    records[devices : devices + NEAR_CAP, :] = near_in[0]
    records[devices + NEAR_CAP : devices + 2 * NEAR_CAP, :] = near_in[1]
    got = records[...]
    slot_of = got[:, dofs + 2 : dofs + 3]
    aim = lax.broadcasted_iota(i32, (got.shape[0], slots), 1).astype(f32) + 1.0
    landing = jnp.where(aim == slot_of, 1.0, 0.0)
    arrived = jnp.dot(
        jnp.transpose(got), landing, precision=HIGHEST, preferred_element_type=f32
    )
    moved = jnp.where(staying, record, 0.0) + arrived
    loads = moved[:dofs]
    coefs = moved[dofs : dofs + 2]
    moved_loads_ref[...] = loads
    moved_coefs_ref[...] = coefs
    first, second = coefs[0:1], coefs[1:2]

    def element_values(both):
        return both[:dofs] * first + both[dofs:] * second

    on_diagonal = lax.broadcasted_iota(i32, (dofs, dofs), 0) == lax.broadcasted_iota(
        i32, (dofs, dofs), 1
    )
    diagonals = [
        jnp.sum(jnp.where(on_diagonal, stiff[k * dofs : (k + 1) * dofs], 0.0), axis=1, keepdims=True)
        for k in range(2)
    ]
    diagonal = scatter(diagonals[0] * first + diagonals[1] * second)
    send_edge(diagonal, 1)
    part = scatter(element_values(both) - loads)
    send_edge(part, 2)
    part_ref[...] = part
    diagonal = receive_edge(diagonal, 1)
    inverse_ref[...] = jnp.where(diagonal > 0.0, 1.0 / diagonal, 0.0)
    residual_ref[...] = jnp.zeros_like(residual_ref)
    update_ref[...] = jnp.zeros_like(update_ref)
    delta_ref[...] = jnp.zeros_like(delta_ref)
    weights = chebyshev_weights()
    table_row = lax.broadcasted_iota(i32, (height, COLUMNS), 0)
    is_owned = lax.rem(table_row, depth) < own_rows

    def next_update(part, old, new):
        residual = residual_ref[...] - part
        return residual, old * update_ref[...] + new * (residual * inverse_ref[...])

    def sweep_step(i, _):
        old, new = jnp.float32(0.0), jnp.float32(0.0)
        for k, (a, b) in enumerate(weights[:-1]):
            old = jnp.where(i == k, a, old)
            new = jnp.where(i == k, b, new)
        part = part_ref[...]
        gather(jnp.where(is_owned, next_update(part, old, new)[1], 0.0))
        residual, update = next_update(receive_edge(part, 2 + i), old, new)
        residual_ref[...] = residual
        update_ref[...] = update
        delta_ref[...] += update
        gather_interface(update)
        part = scatter(element_values(products()))
        send_edge(part, 3 + i)
        part_ref[...] = part
        return 0

    lax.fori_loop(0, len(weights) - 1, sweep_step, 0)

    part = receive_edge(part_ref[...], 1 + len(weights))
    delta = delta_ref[...] + next_update(part, *weights[-1])[1]
    result = start_table[...] + delta + move_faces(delta, 1, 0)
    for r in range(own_rows):
        for c in range(components):
            out_ref[c : c + 1, r * COLUMNS : (r + 1) * COLUMNS] = result[
                c * depth + r : c * depth + r + 1
            ]

    sent([near_copy(0), near_copy(1)])

    def far_sent(d, _):
        far_copy(lax.rem(me + d, devices), me).wait_send()
        return 0

    lax.fori_loop(1, devices, far_sent, 0)

    def edge_sent(t, _):
        sent([edge_copy(0, t), edge_copy(1, t)])
        return 0

    lax.fori_loop(0, edges, edge_sent, 0)


def local(
    devices, subs,
    start_field, element_loads, element_coefs, element_nodes, move_list, face_nodes, stiffness,
):
    dofs, slots = element_loads.shape
    per_element = element_nodes.shape[0]
    components = dofs // per_element
    owned = start_field.shape[1]
    face = face_nodes.shape[1]
    extra_rows = 4 * face // COLUMNS
    own_rows = owned // COLUMNS
    assert owned % COLUMNS == 0 and 4 * face == 3 * COLUMNS and own_rows % TILE + 3 <= TILE
    depth = -(-(own_rows + extra_rows) // TILE) * TILE
    table = (components * depth, COLUMNS)
    groups = per_element // GROUP
    rows = -(-(devices + 2 * NEAR_CAP) // LANES) * LANES
    edges = 2 + SWEEPS * DEGREE
    vmem = pl.BlockSpec(memory_space=pltpu.VMEM)
    smem = pl.BlockSpec(memory_space=pltpu.SMEM)
    anywhere = pl.BlockSpec(memory_space=pl.ANY)
    return pl.pallas_call(
        functools.partial(kernel, devices, subs),
        out_shape=(
            jax.ShapeDtypeStruct(start_field.shape, f32),
            jax.ShapeDtypeStruct((dofs, slots), f32),
            jax.ShapeDtypeStruct((2, slots), f32),
        ),
        in_specs=[anywhere, anywhere, vmem, anywhere, vmem, smem, vmem, anywhere],
        out_specs=(vmem, vmem, vmem),
        scratch_shapes=[
            pltpu.VMEM(start_field.shape, f32),
            pltpu.VMEM((dofs, slots), f32),
            pltpu.VMEM((per_element, slots), i32),
            pltpu.VMEM((2 * dofs, dofs), f32),
            pltpu.SemaphoreType.DMA((4,)),
            pltpu.VMEM((per_element, COLUMNS, slots), bf16),
            pltpu.VMEM((per_element * slots, COLUMNS), bf16),
            pltpu.VMEM((groups, slots, GROUP), f32),
            pltpu.VMEM((per_element, slots), i32),
            pltpu.VMEM((per_element, slots), i32),
            pltpu.VMEM((per_element, slots), i32),
            pltpu.VMEM((2 * dofs, dofs), bf16),
            pltpu.VMEM((2 * dofs, dofs), bf16),
            pltpu.VMEM((dofs, slots), f32),
            pltpu.VMEM((dofs, slots), f32),
            pltpu.VMEM(table, f32),
            pltpu.VMEM(table, f32),
            pltpu.VMEM(table, f32),
            pltpu.VMEM(table, f32),
            pltpu.VMEM(table, f32),
            pltpu.VMEM(table, f32),
            pltpu.VMEM((2 * table[0], COLUMNS), f32),
            pltpu.VMEM((devices, 1, slots), f32),
            pltpu.VMEM((devices, 1, slots), f32),
            pltpu.VMEM((2, NEAR_CAP, slots), f32),
            pltpu.VMEM((2, NEAR_CAP, slots), f32),
            pltpu.VMEM((rows, slots), f32),
            pltpu.VMEM((2, edges, components, TILE, LANES), f32),
            pltpu.VMEM((2, edges, components, TILE, LANES), f32),
            pltpu.SemaphoreType.DMA((devices,)),
            pltpu.SemaphoreType.DMA((devices,)),
            pltpu.SemaphoreType.DMA((2,)),
            pltpu.SemaphoreType.DMA((2,)),
            pltpu.SemaphoreType.DMA((2, edges)),
            pltpu.SemaphoreType.DMA((2, edges)),
        ],
        compiler_params=pltpu.CompilerParams(
            collective_id=0, has_side_effects=True, vmem_limit_bytes=56 * 1024 * 1024
        ),
        name="migrate_and_smooth",
    )(
        start_field,
        element_loads,
        element_coefs,
        element_nodes,
        move_list,
        face_nodes,
        face_nodes,
        stiffness.reshape(2 * dofs, dofs),
    )


def solution(mesh):
    devices = mesh.shape["seg"] * mesh.shape["sub"]
    return jax.shard_map(
        functools.partial(local, devices, mesh.shape["sub"]),
        mesh=mesh,
        in_specs=(
            P(None, ("seg", "sub")),
            P(None, ("seg", "sub")),
            P(None, ("seg", "sub")),
            P(None, ("seg", "sub")),
            P(None, ("seg", "sub")),
            P(None, ("seg", "sub")),
            P(),
        ),
        out_specs=(P(None, ("seg", "sub")), P(None, ("seg", "sub")), P(None, ("seg", "sub"))),
        check_vma=False,
    )
```

```python
import functools

import jax
import jax.numpy as jnp
from jax import lax
from jax.experimental import pallas as pl
from jax.experimental.pallas import tpu as pltpu
from jax.sharding import PartitionSpec as P

NEAR_CAP = 16
DEGREE = 4
SWEEPS = 2
COLUMNS = 256
TILE = 8
GROUP = 8
LANES = 128
UNROLL = 4
GATHER_UNROLL = 3

center = 1.125
half_width = 0.875

f32 = jnp.float32
bf16 = jnp.bfloat16
i32 = jnp.int32
HIGHEST = lax.Precision.HIGHEST


def chebyshev_weights():
    weights = []
    scaled_center = center / half_width
    for _ in range(SWEEPS):
        weights.append((0.0, 1.0 / center))
        ratio = 1.0 / scaled_center
        for _ in range(DEGREE - 1):
            ratio_next = 1.0 / (2.0 * scaled_center - ratio)
            weights.append((ratio_next * ratio, 2.0 * ratio_next / half_width))
            ratio = ratio_next
    return weights


def split(x):
    high = x.astype(bf16)
    return high, (x - high.astype(f32)).astype(bf16)


def dot(a, b):
    return jnp.dot(a, b, preferred_element_type=f32)


def dot_nt(a, b, precision=None):
    return lax.dot_general(
        a, b, (((1,), (1,)), ((), ())), precision=precision, preferred_element_type=f32
    )


def pick_low(found, low_row, components):
    half = found.shape[0] // 2
    depth = half // components
    mask = lax.broadcasted_iota(i32, (depth, low_row.shape[1]), 0) == low_row
    both = found[:half] + found[half:]
    return [
        jnp.sum(jnp.where(mask, both[c * depth : (c + 1) * depth], 0.0), axis=0, keepdims=True)
        for c in range(components)
    ]


def spread_low(rows, low_row, first, last):
    mask = lax.broadcasted_iota(i32, (last - first, low_row.shape[1]), 0) == low_row - first
    tall = []
    for part in range(2):
        for row in rows:
            high = row.astype(bf16).astype(f32)
            piece = high if part == 0 else row - high
            tall.append(jnp.where(mask, piece, 0.0).astype(bf16))
    return jnp.concatenate(tall, axis=0)


def one_hot_rows(row, count):
    numbers = lax.broadcasted_iota(i32, (count, row.shape[1]), 0).astype(f32).astype(bf16)
    hit = numbers == row.astype(f32).astype(bf16)
    return jnp.where(hit, jnp.ones_like(numbers), jnp.zeros_like(numbers))


def kernel(
    devices, subs,
    start_hbm, loads_hbm, coefs_ref, nodes_hbm, moves_ref, face_smem, face_ref, stiff_hbm,
    out_ref, moved_loads_ref, moved_coefs_ref,
    start_ref, loads_ref, nodes_ref, stiff_ref, arrive,
    onehot_t, column_t, low_ref, place_ref, stiff_high, stiff_low, x_ref, y_ref,
    start_table, update_ref, residual_ref, inverse_ref, delta_ref, part_ref, early_ref, total_ref,
    far_out, far_in, near_out, near_in, records, edge_out, edge_in,
    far_send, far_recv, near_send, near_recv, edge_send, edge_recv,
):
    per_element, slots = nodes_ref.shape
    dofs = loads_ref.shape[0]
    components = dofs // per_element
    owned = start_ref.shape[1]
    face = face_ref.shape[1]
    height = start_table.shape[0]
    depth = height // components
    own_rows = owned // COLUMNS
    edges = edge_out.shape[1]
    groups = per_element // GROUP
    me = lax.axis_index("seg") * subs + lax.axis_index("sub")
    has_prev = me > 0
    has_next = me < devices - 1

    incoming = [
        pltpu.make_async_copy(source, target, arrive.at[k])
        for k, (source, target) in enumerate(
            [(loads_hbm, loads_ref), (start_hbm, start_ref), (nodes_hbm, nodes_ref), (stiff_hbm, stiff_ref)]
        )
    ]
    for copy in incoming:
        copy.start()

    def coords(p):
        return {"seg": lax.div(p, subs), "sub": lax.rem(p, subs)}

    before = coords(jnp.maximum(me - 1, 0))
    after = coords(jnp.minimum(me + 1, devices - 1))

    far_in[me] = jnp.zeros((1, slots), f32)
    near_in[...] = jnp.zeros_like(near_in)
    barrier = pltpu.get_barrier_semaphore()

    def greet(d, _):
        pl.semaphore_signal(
            barrier, inc=1, device_id=coords(lax.rem(me + d, devices)),
            device_id_type=pl.DeviceIdType.MESH,
        )
        return 0

    lax.fori_loop(1, devices, greet, 0)

    def edge_copy(way, t):
        return pltpu.make_async_remote_copy(
            src_ref=edge_out.at[way, t], dst_ref=edge_in.at[way, t],
            send_sem=edge_send.at[way, t], recv_sem=edge_recv.at[way, t],
            device_id=after if way == 0 else before, device_id_type=pl.DeviceIdType.MESH,
        )

    def near_copy(way):
        return pltpu.make_async_remote_copy(
            src_ref=near_out.at[way], dst_ref=near_in.at[way],
            send_sem=near_send.at[way], recv_sem=near_recv.at[way],
            device_id=after if way == 0 else before, device_id_type=pl.DeviceIdType.MESH,
        )

    def both_ways(copies):
        @pl.when(has_next)
        def _():
            copies[0].start()

        @pl.when(has_prev)
        def _():
            copies[1].start()

    def receive(copies):
        @pl.when(has_prev)
        def _():
            copies[0].wait_recv()

        @pl.when(has_next)
        def _():
            copies[1].wait_recv()

    def sent(copies):
        @pl.when(has_next)
        def _():
            copies[0].wait_send()

        @pl.when(has_prev)
        def _():
            copies[1].wait_send()

    top = own_rows % TILE
    tile_at = own_rows - top
    sublane = lax.broadcasted_iota(i32, (TILE, LANES), 0)

    def send_edge(part, t):
        for c in range(components):
            at = c * TILE
            left, right = part[at : at + TILE, :LANES], part[at : at + TILE, LANES:]
            edge_out[0, t, c] = jnp.where(sublane == top + 2, pltpu.roll(right, 2, 0), left)
            edge_out[1, t, c] = jnp.where(sublane == top, pltpu.roll(left, TILE - 2, 0), right)
        both_ways([edge_copy(0, t), edge_copy(1, t)])

    first_row, middle_row, last_row = (sublane == top + k for k in range(3))

    def receive_edge(part, t):
        receive([edge_copy(0, t), edge_copy(1, t)])
        pieces = []
        for c in range(components):
            at = c * depth + tile_at
            left, right = part[at : at + TILE, :LANES], part[at : at + TILE, LANES:]
            prev, next_ = edge_in[0, t, c], edge_in[1, t, c]
            shifted = pltpu.roll(next_, TILE - 1, 0)
            left = left + jnp.where(
                last_row & has_prev, prev, jnp.where((first_row | middle_row) & has_next, shifted, 0.0)
            )
            shifted = pltpu.roll(prev, 1, 0)
            right = right + jnp.where(
                first_row & has_next, next_, jnp.where((middle_row | last_row) & has_prev, shifted, 0.0)
            )
            pieces += [
                part[c * depth : at], jnp.concatenate([left, right], axis=1),
                part[at + TILE : (c + 1) * depth],
            ]
        return jnp.concatenate([piece for piece in pieces if piece.shape[0]], axis=0)

    lists = []
    for k in range(2):
        old = face_ref[1 - k : 2 - k, :]
        new = owned + (1 + k) * face + lax.broadcasted_iota(i32, (1, face), 1)
        lists.append(
            [(node >> 8, one_hot_rows(node & (COLUMNS - 1), COLUMNS)) for node in (old, new)]
        )

    def move_faces(values, source, target):
        both = jnp.concatenate(split(values), axis=0)
        total = 0.0
        for places in lists:
            low, hot = places[source]
            rows = pick_low(dot(both, hot), low, components)
            low, hot = places[target]
            total = total + dot_nt(spread_low(rows, low, 0, depth), hot)
        return total[:height] + total[height:]

    incoming[0].wait()
    incoming[1].wait()
    start_table[...] = jnp.zeros_like(start_table)
    for r in range(own_rows):
        for c in range(components):
            start_table[c * depth + r : c * depth + r + 1, :] = start_ref[
                c : c + 1, r * COLUMNS : (r + 1) * COLUMNS
            ]
    start = start_table[...]
    field = start + move_faces(start, 0, 1)

    dest = moves_ref[0:1, :]
    new_slot = moves_ref[1:2, :]
    spot = moves_ref[2:3, :]
    staying = dest == me
    row_of = jnp.where(
        dest == me + 1, devices + spot,
        jnp.where(dest == me - 1, devices + NEAR_CAP + spot, dest),
    )
    row_of = jnp.where(staying, -1, row_of)
    record = jnp.concatenate(
        [
            loads_ref[...], coefs_ref[...], (new_slot + 1).astype(f32),
            jnp.zeros((slots - dofs - 3, slots), f32),
        ],
        axis=0,
    )
    rows = devices + 2 * NEAR_CAP
    chosen = lax.broadcasted_iota(i32, (rows, slots), 0) == row_of
    packed = dot_nt(jnp.where(chosen, 1.0, 0.0), record, HIGHEST)
    for p in range(devices):
        far_out[p] = packed[p : p + 1]
    near_out[0] = packed[devices : devices + NEAR_CAP]
    near_out[1] = packed[devices + NEAR_CAP :]

    def far_copy(p, row):
        return pltpu.make_async_remote_copy(
            src_ref=far_out.at[p], dst_ref=far_in.at[row],
            send_sem=far_send.at[p], recv_sem=far_recv.at[row],
            device_id=coords(p), device_id_type=pl.DeviceIdType.MESH,
        )

    pl.semaphore_wait(barrier, devices - 1)
    send_edge(
        jnp.concatenate(
            [field[c * depth + tile_at : (c + 1) * depth] for c in range(components)], axis=0
        ),
        0,
    )
    both_ways([near_copy(0), near_copy(1)])

    def far_start(d, _):
        far_copy(lax.rem(me + d, devices), me).start()
        return 0

    lax.fori_loop(1, devices, far_start, 0)

    incoming[2].wait()
    nodes = nodes_ref[...]
    place = jnp.where(
        nodes < owned, nodes, jnp.where(nodes < owned + face, nodes + 3 * face, nodes - face)
    )

    def relabel(s, place):
        place = jnp.where(nodes == face_smem[1, s], owned + face + s, place)
        return jnp.where(nodes == face_smem[0, s], owned + 2 * face + s, place)

    place = lax.fori_loop(0, face, relabel, place, unroll=8)
    low_ref[...] = place >> 8
    column = place & (COLUMNS - 1)
    place_ref[...] = place
    column_rows = jnp.transpose(column.astype(f32))
    for g in range(groups):
        column_t[g] = column_rows[:, g * GROUP : (g + 1) * GROUP]

    def build(g, _):
        own = column_t[g].astype(bf16)
        numbers = lax.broadcasted_iota(i32, (slots, COLUMNS), 1).astype(f32).astype(bf16)
        for j in range(GROUP):
            n = g * GROUP + j
            hit = numbers == own[:, j : j + 1]
            onehot_t[pl.ds(pl.multiple_of(n * slots, slots), slots), :] = jnp.where(
                hit, jnp.ones_like(numbers), jnp.zeros_like(numbers)
            )
        return 0

    lax.fori_loop(0, groups, build, 0)

    incoming[3].wait()
    stiff = stiff_ref[...]
    stiff_high[...] = stiff.astype(bf16)
    stiff_low[...] = (stiff - stiff_high[...].astype(f32)).astype(bf16)

    def gather(table_ref, first, last, found_of, unroll):
        for side in range(slots // LANES):
            lanes = slice(side * LANES, (side + 1) * LANES)
            place = place_ref[:, lanes]
            lane_of = place & (LANES - 1)
            piece_of = place >> 7

            def step(r, found):
                lines = [table_ref[pl.ds(c * depth + r, 1), :] for c in range(components)]
                for half in range(2):
                    hit = piece_of == 2 * r + half
                    taken = []
                    for c in range(components):
                        line = lines[c][:, half * LANES : (half + 1) * LANES]
                        line = jnp.broadcast_to(line, (per_element, LANES))
                        line = jnp.take_along_axis(line, lane_of, axis=1, mode="promise_in_bounds")
                        taken.append(jnp.where(hit, line, found[c]))
                    found = tuple(taken)
                return found

            rows = [slice(c * per_element, (c + 1) * per_element) for c in range(components)]
            found = tuple(found_of(row, lanes) for row in rows)
            found = lax.fori_loop(first, last, step, found, unroll=unroll)
            for c in range(components):
                x_ref[rows[c], lanes] = found[c]

    def gather_owned(table_ref):
        gather(
            table_ref, 0, own_rows, lambda row, lanes: jnp.zeros((per_element, LANES), f32), GATHER_UNROLL
        )

    def gather_interface(table_ref):
        gather(table_ref, own_rows, own_rows + 3, lambda row, lanes: x_ref[row, lanes], True)

    def scatter_rows(first, last):
        count = 2 * components * (last - first)
        total_ref[:count] = jnp.zeros((count, COLUMNS), f32)

        def step(g, _):
            low8 = low_ref[pl.ds(pl.multiple_of(g * GROUP, GROUP), GROUP), :]
            parts = [
                y_ref[pl.ds(pl.multiple_of(c * per_element + g * GROUP, GROUP), GROUP), :]
                for c in range(components)
            ]
            wide = jnp.concatenate(
                [
                    spread_low([part[j : j + 1] for part in parts], low8[j : j + 1], first, last)
                    for j in range(GROUP)
                ],
                axis=1,
            )
            at = pl.multiple_of(g * GROUP * slots, GROUP * slots)
            total_ref[:count] += dot(wide, onehot_t[pl.ds(at, GROUP * slots), :])
            return 0

        lax.fori_loop(0, groups, step, 0, unroll=UNROLL)
        return total_ref[: count // 2] + total_ref[count // 2 : count]

    def scatter(values, t):
        y_ref[...] = values
        edge = scatter_rows(tile_at, depth)
        send_edge(edge, t)
        rest = scatter_rows(0, tile_at)
        pieces = []
        for c in range(components):
            pieces += [rest[c * tile_at : (c + 1) * tile_at], edge[c * TILE : (c + 1) * TILE]]
        return jnp.concatenate(pieces, axis=0)

    def products():
        x_high, x_low = split(x_ref[...])
        return dot(stiff_high[...], x_high) + (
            dot(stiff_low[...], x_high) + dot(stiff_high[...], x_low)
        )

    gather_owned(start_table)
    update_ref[...] = receive_edge(field, 0)
    gather_interface(update_ref)
    both = products()

    receive([near_copy(0), near_copy(1)])

    def far_finish(d, _):
        p = lax.rem(me + d, devices)
        far_copy(p, p).wait_recv()
        return 0

    lax.fori_loop(1, devices, far_finish, 0)
    records[...] = jnp.zeros_like(records)
    for p in range(devices):
        records[p : p + 1, :] = far_in[p]
    records[devices : devices + NEAR_CAP, :] = near_in[0]
    records[devices + NEAR_CAP : devices + 2 * NEAR_CAP, :] = near_in[1]
    got = records[...]
    slot_of = got[:, dofs + 2 : dofs + 3]
    aim = lax.broadcasted_iota(i32, (got.shape[0], slots), 1).astype(f32) + 1.0
    landing = jnp.where(aim == slot_of, 1.0, 0.0)
    arrived = jnp.dot(
        jnp.transpose(got), landing, precision=HIGHEST, preferred_element_type=f32
    )
    moved = jnp.where(staying, record, 0.0) + arrived
    loads = moved[:dofs]
    coefs = moved[dofs : dofs + 2]
    moved_loads_ref[...] = loads
    moved_coefs_ref[...] = coefs
    first, second = coefs[0:1], coefs[1:2]

    def element_values(both):
        return both[:dofs] * first + both[dofs:] * second

    on_diagonal = lax.broadcasted_iota(i32, (dofs, dofs), 0) == lax.broadcasted_iota(
        i32, (dofs, dofs), 1
    )
    diagonals = [
        jnp.sum(jnp.where(on_diagonal, stiff[k * dofs : (k + 1) * dofs], 0.0), axis=1, keepdims=True)
        for k in range(2)
    ]
    diagonal = scatter(diagonals[0] * first + diagonals[1] * second, 1)
    part_ref[...] = scatter(element_values(both) - loads, 2)
    diagonal = receive_edge(diagonal, 1)
    inverse_ref[...] = jnp.where(diagonal > 0.0, 1.0 / diagonal, 0.0)
    residual_ref[...] = jnp.zeros_like(residual_ref)
    update_ref[...] = jnp.zeros_like(update_ref)
    delta_ref[...] = jnp.zeros_like(delta_ref)
    weights = chebyshev_weights()

    def next_update(part, old, new):
        residual = residual_ref[...] - part
        return residual, old * update_ref[...] + new * (residual * inverse_ref[...])

    def sweep_step(i, _):
        old, new = jnp.float32(0.0), jnp.float32(0.0)
        for k, (a, b) in enumerate(weights[:-1]):
            old = jnp.where(i == k, a, old)
            new = jnp.where(i == k, b, new)
        part = part_ref[...]
        early_ref[...] = next_update(part, old, new)[1]
        gather_owned(early_ref)
        residual, update = next_update(receive_edge(part, 2 + i), old, new)
        residual_ref[...] = residual
        update_ref[...] = update
        delta_ref[...] += update
        gather_interface(update_ref)
        part_ref[...] = scatter(element_values(products()), 3 + i)
        return 0

    lax.fori_loop(0, len(weights) - 1, sweep_step, 0)

    part = receive_edge(part_ref[...], 1 + len(weights))
    delta = delta_ref[...] + next_update(part, *weights[-1])[1]
    result = start_table[...] + delta + move_faces(delta, 1, 0)
    for r in range(own_rows):
        for c in range(components):
            out_ref[c : c + 1, r * COLUMNS : (r + 1) * COLUMNS] = result[
                c * depth + r : c * depth + r + 1
            ]

    sent([near_copy(0), near_copy(1)])

    def far_sent(d, _):
        far_copy(lax.rem(me + d, devices), me).wait_send()
        return 0

    lax.fori_loop(1, devices, far_sent, 0)

    def edge_sent(t, _):
        sent([edge_copy(0, t), edge_copy(1, t)])
        return 0

    lax.fori_loop(0, edges, edge_sent, 0)


def local(
    devices, subs,
    start_field, element_loads, element_coefs, element_nodes, move_list, face_nodes, stiffness,
):
    dofs, slots = element_loads.shape
    per_element = element_nodes.shape[0]
    components = dofs // per_element
    owned = start_field.shape[1]
    face = face_nodes.shape[1]
    extra_rows = 4 * face // COLUMNS
    own_rows = owned // COLUMNS
    assert owned % COLUMNS == 0 and 4 * face == 3 * COLUMNS and own_rows % TILE + 3 <= TILE
    depth = -(-(own_rows + extra_rows) // TILE) * TILE
    table = (components * depth, COLUMNS)
    groups = per_element // GROUP
    rows = -(-(devices + 2 * NEAR_CAP) // LANES) * LANES
    edges = 2 + SWEEPS * DEGREE
    vmem = pl.BlockSpec(memory_space=pltpu.VMEM)
    smem = pl.BlockSpec(memory_space=pltpu.SMEM)
    anywhere = pl.BlockSpec(memory_space=pl.ANY)
    return pl.pallas_call(
        functools.partial(kernel, devices, subs),
        out_shape=(
            jax.ShapeDtypeStruct(start_field.shape, f32),
            jax.ShapeDtypeStruct((dofs, slots), f32),
            jax.ShapeDtypeStruct((2, slots), f32),
        ),
        in_specs=[anywhere, anywhere, vmem, anywhere, vmem, smem, vmem, anywhere],
        out_specs=(vmem, vmem, vmem),
        scratch_shapes=[
            pltpu.VMEM(start_field.shape, f32),
            pltpu.VMEM((dofs, slots), f32),
            pltpu.VMEM((per_element, slots), i32),
            pltpu.VMEM((2 * dofs, dofs), f32),
            pltpu.SemaphoreType.DMA((4,)),
            pltpu.VMEM((per_element * slots, COLUMNS), bf16),
            pltpu.VMEM((groups, slots, GROUP), f32),
            pltpu.VMEM((per_element, slots), i32),
            pltpu.VMEM((per_element, slots), i32),
            pltpu.VMEM((2 * dofs, dofs), bf16),
            pltpu.VMEM((2 * dofs, dofs), bf16),
            pltpu.VMEM((dofs, slots), f32),
            pltpu.VMEM((dofs, slots), f32),
            pltpu.VMEM(table, f32),
            pltpu.VMEM(table, f32),
            pltpu.VMEM(table, f32),
            pltpu.VMEM(table, f32),
            pltpu.VMEM(table, f32),
            pltpu.VMEM(table, f32),
            pltpu.VMEM(table, f32),
            pltpu.VMEM((2 * table[0], COLUMNS), f32),
            pltpu.VMEM((devices, 1, slots), f32),
            pltpu.VMEM((devices, 1, slots), f32),
            pltpu.VMEM((2, NEAR_CAP, slots), f32),
            pltpu.VMEM((2, NEAR_CAP, slots), f32),
            pltpu.VMEM((rows, slots), f32),
            pltpu.VMEM((2, edges, components, TILE, LANES), f32),
            pltpu.VMEM((2, edges, components, TILE, LANES), f32),
            pltpu.SemaphoreType.DMA((devices,)),
            pltpu.SemaphoreType.DMA((devices,)),
            pltpu.SemaphoreType.DMA((2,)),
            pltpu.SemaphoreType.DMA((2,)),
            pltpu.SemaphoreType.DMA((2, edges)),
            pltpu.SemaphoreType.DMA((2, edges)),
        ],
        compiler_params=pltpu.CompilerParams(
            collective_id=0, has_side_effects=True, vmem_limit_bytes=56 * 1024 * 1024
        ),
        name="migrate_and_smooth",
    )(
        start_field,
        element_loads,
        element_coefs,
        element_nodes,
        move_list,
        face_nodes,
        face_nodes,
        stiffness.reshape(2 * dofs, dofs),
    )


def solution(mesh):
    devices = mesh.shape["seg"] * mesh.shape["sub"]
    return jax.shard_map(
        functools.partial(local, devices, mesh.shape["sub"]),
        mesh=mesh,
        in_specs=(
            P(None, ("seg", "sub")),
            P(None, ("seg", "sub")),
            P(None, ("seg", "sub")),
            P(None, ("seg", "sub")),
            P(None, ("seg", "sub")),
            P(None, ("seg", "sub")),
            P(),
        ),
        out_specs=(P(None, ("seg", "sub")), P(None, ("seg", "sub")), P(None, ("seg", "sub"))),
        check_vma=False,
    )
```

```python
import functools

import jax
import jax.numpy as jnp
from jax import lax
from jax.experimental import pallas as pl
from jax.experimental.pallas import tpu as pltpu
from jax.sharding import PartitionSpec as P

NEAR_CAP = 16
DEGREE = 4
SWEEPS = 2
COLUMNS = 256
TILE = 8
GROUP = 8
LANES = 128
UNROLL = 8

center = 1.125
half_width = 0.875

f32 = jnp.float32
bf16 = jnp.bfloat16
i32 = jnp.int32
HIGHEST = lax.Precision.HIGHEST


def chebyshev_weights():
    weights = []
    scaled_center = center / half_width
    for _ in range(SWEEPS):
        weights.append((0.0, 1.0 / center))
        ratio = 1.0 / scaled_center
        for _ in range(DEGREE - 1):
            ratio_next = 1.0 / (2.0 * scaled_center - ratio)
            weights.append((ratio_next * ratio, 2.0 * ratio_next / half_width))
            ratio = ratio_next
    return weights


def split(x):
    high = x.astype(bf16)
    return high, (x - high.astype(f32)).astype(bf16)


def dot(a, b):
    return jnp.dot(a, b, preferred_element_type=f32)


def dot_nt(a, b, precision=None):
    return lax.dot_general(
        a, b, (((1,), (1,)), ((), ())), precision=precision, preferred_element_type=f32
    )


def pick_low(found, low_row, components):
    half = found.shape[0] // 2
    depth = half // components
    mask = lax.broadcasted_iota(i32, (depth, low_row.shape[1]), 0) == low_row
    both = found[:half] + found[half:]
    return [
        jnp.sum(jnp.where(mask, both[c * depth : (c + 1) * depth], 0.0), axis=0, keepdims=True)
        for c in range(components)
    ]


def spread_low(rows, low_row, depth):
    mask = low_mask(low_row, depth)
    tall = []
    for part in range(2):
        for row in rows:
            high = row.astype(bf16).astype(f32)
            piece = high if part == 0 else row - high
            piece = jnp.broadcast_to(piece, (2 * TILE, row.shape[1])).astype(bf16)
            piece = jnp.concatenate([piece] * (depth // (2 * TILE)), axis=0)
            tall.append(jnp.where(mask, piece, jnp.zeros_like(piece)))
    return jnp.concatenate(tall, axis=0)


def low_mask(low_row, depth):
    numbers = lax.broadcasted_iota(i32, (depth, low_row.shape[1]), 0).astype(f32).astype(bf16)
    return numbers == low_row.astype(f32).astype(bf16)


def one_hot_rows(row, count):
    numbers = lax.broadcasted_iota(i32, (count, row.shape[1]), 0).astype(f32).astype(bf16)
    hit = numbers == row.astype(f32).astype(bf16)
    return jnp.where(hit, jnp.ones_like(numbers), jnp.zeros_like(numbers))


def kernel(
    devices, subs,
    start_hbm, loads_hbm, coefs_ref, nodes_hbm, moves_ref, face_smem, face_ref, stiff_hbm,
    out_ref, moved_loads_ref, moved_coefs_ref,
    start_ref, loads_ref, nodes_ref, stiff_ref, arrive,
    onehot, onehot_t, column_t, low_ref, high_ref, extra_ref, stiff_high, stiff_low, x_ref, y_ref,
    start_table, update_ref, residual_ref, inverse_ref, delta_ref, part_ref, total_ref,
    far_out, far_in, near_out, near_in, records, edge_out, edge_in,
    far_send, far_recv, near_send, near_recv, edge_send, edge_recv,
):
    per_element, slots = nodes_ref.shape
    dofs = loads_ref.shape[0]
    components = dofs // per_element
    owned = start_ref.shape[1]
    face = face_ref.shape[1]
    height = start_table.shape[0]
    depth = height // components
    own_rows = owned // COLUMNS
    edges = edge_out.shape[1]
    groups = per_element // GROUP
    me = lax.axis_index("seg") * subs + lax.axis_index("sub")
    has_prev = me > 0
    has_next = me < devices - 1

    incoming = [
        pltpu.make_async_copy(source, target, arrive.at[k])
        for k, (source, target) in enumerate(
            [(loads_hbm, loads_ref), (start_hbm, start_ref), (nodes_hbm, nodes_ref), (stiff_hbm, stiff_ref)]
        )
    ]
    for copy in incoming:
        copy.start()

    def coords(p):
        return {"seg": lax.div(p, subs), "sub": lax.rem(p, subs)}

    before = coords(jnp.maximum(me - 1, 0))
    after = coords(jnp.minimum(me + 1, devices - 1))

    far_in[me] = jnp.zeros((1, slots), f32)
    near_in[...] = jnp.zeros_like(near_in)
    barrier = pltpu.get_barrier_semaphore()

    def greet(d, _):
        pl.semaphore_signal(
            barrier, inc=1, device_id=coords(lax.rem(me + d, devices)),
            device_id_type=pl.DeviceIdType.MESH,
        )
        return 0

    lax.fori_loop(1, devices, greet, 0)

    def edge_copy(way, t):
        return pltpu.make_async_remote_copy(
            src_ref=edge_out.at[way, t], dst_ref=edge_in.at[way, t],
            send_sem=edge_send.at[way, t], recv_sem=edge_recv.at[way, t],
            device_id=after if way == 0 else before, device_id_type=pl.DeviceIdType.MESH,
        )

    def near_copy(way):
        return pltpu.make_async_remote_copy(
            src_ref=near_out.at[way], dst_ref=near_in.at[way],
            send_sem=near_send.at[way], recv_sem=near_recv.at[way],
            device_id=after if way == 0 else before, device_id_type=pl.DeviceIdType.MESH,
        )

    def both_ways(copies):
        @pl.when(has_next)
        def _():
            copies[0].start()

        @pl.when(has_prev)
        def _():
            copies[1].start()

    def receive(copies):
        @pl.when(has_prev)
        def _():
            copies[0].wait_recv()

        @pl.when(has_next)
        def _():
            copies[1].wait_recv()

    def sent(copies):
        @pl.when(has_next)
        def _():
            copies[0].wait_send()

        @pl.when(has_prev)
        def _():
            copies[1].wait_send()

    top = own_rows % TILE
    tile_at = own_rows - top
    sublane = lax.broadcasted_iota(i32, (TILE, LANES), 0)

    def send_edge(part, t):
        for c in range(components):
            at = c * depth + tile_at
            left, right = part[at : at + TILE, :LANES], part[at : at + TILE, LANES:]
            edge_out[0, t, c] = jnp.where(sublane == top + 2, pltpu.roll(right, 2, 0), left)
            edge_out[1, t, c] = jnp.where(sublane == top, pltpu.roll(left, TILE - 2, 0), right)
        both_ways([edge_copy(0, t), edge_copy(1, t)])

    first_row, middle_row, last_row = (sublane == top + k for k in range(3))

    def receive_edge(part, t):
        receive([edge_copy(0, t), edge_copy(1, t)])
        pieces = []
        for c in range(components):
            at = c * depth + tile_at
            left, right = part[at : at + TILE, :LANES], part[at : at + TILE, LANES:]
            prev, next_ = edge_in[0, t, c], edge_in[1, t, c]
            shifted = pltpu.roll(next_, TILE - 1, 0)
            left = left + jnp.where(
                last_row & has_prev, prev, jnp.where((first_row | middle_row) & has_next, shifted, 0.0)
            )
            shifted = pltpu.roll(prev, 1, 0)
            right = right + jnp.where(
                first_row & has_next, next_, jnp.where((middle_row | last_row) & has_prev, shifted, 0.0)
            )
            pieces += [
                part[c * depth : at], jnp.concatenate([left, right], axis=1),
                part[at + TILE : (c + 1) * depth],
            ]
        return jnp.concatenate([piece for piece in pieces if piece.shape[0]], axis=0)

    lists = []
    for k in range(2):
        old = face_ref[1 - k : 2 - k, :]
        new = owned + (1 + k) * face + lax.broadcasted_iota(i32, (1, face), 1)
        lists.append(
            [(node >> 8, one_hot_rows(node & (COLUMNS - 1), COLUMNS)) for node in (old, new)]
        )

    def move_faces(values, source, target):
        both = jnp.concatenate(split(values), axis=0)
        total = 0.0
        for places in lists:
            low, hot = places[source]
            rows = pick_low(dot(both, hot), low, components)
            low, hot = places[target]
            total = total + dot_nt(spread_low(rows, low, depth), hot)
        return total[:height] + total[height:]

    incoming[0].wait()
    incoming[1].wait()
    start_table[...] = jnp.zeros_like(start_table)
    for r in range(own_rows):
        for c in range(components):
            start_table[c * depth + r : c * depth + r + 1, :] = start_ref[
                c : c + 1, r * COLUMNS : (r + 1) * COLUMNS
            ]
    start = start_table[...]
    field = start + move_faces(start, 0, 1)

    dest = moves_ref[0:1, :]
    new_slot = moves_ref[1:2, :]
    spot = moves_ref[2:3, :]
    staying = dest == me
    row_of = jnp.where(
        dest == me + 1, devices + spot,
        jnp.where(dest == me - 1, devices + NEAR_CAP + spot, dest),
    )
    row_of = jnp.where(staying, -1, row_of)
    record = jnp.concatenate(
        [
            loads_ref[...], coefs_ref[...], (new_slot + 1).astype(f32),
            jnp.zeros((slots - dofs - 3, slots), f32),
        ],
        axis=0,
    )
    rows = devices + 2 * NEAR_CAP
    chosen = lax.broadcasted_iota(i32, (rows, slots), 0) == row_of
    packed = dot_nt(jnp.where(chosen, 1.0, 0.0), record, HIGHEST)
    for p in range(devices):
        far_out[p] = packed[p : p + 1]
    near_out[0] = packed[devices : devices + NEAR_CAP]
    near_out[1] = packed[devices + NEAR_CAP :]

    def far_copy(p, row):
        return pltpu.make_async_remote_copy(
            src_ref=far_out.at[p], dst_ref=far_in.at[row],
            send_sem=far_send.at[p], recv_sem=far_recv.at[row],
            device_id=coords(p), device_id_type=pl.DeviceIdType.MESH,
        )

    pl.semaphore_wait(barrier, devices - 1)
    send_edge(field, 0)
    both_ways([near_copy(0), near_copy(1)])

    def far_start(d, _):
        far_copy(lax.rem(me + d, devices), me).start()
        return 0

    lax.fori_loop(1, devices, far_start, 0)

    incoming[2].wait()
    nodes = nodes_ref[...]
    place = jnp.where(
        nodes < owned, nodes, jnp.where(nodes < owned + face, nodes + 3 * face, nodes - face)
    )

    def relabel(s, place):
        place = jnp.where(nodes == face_smem[1, s], owned + face + s, place)
        return jnp.where(nodes == face_smem[0, s], owned + 2 * face + s, place)

    place = lax.fori_loop(0, face, relabel, place, unroll=8)
    low_ref[...] = place >> 8
    column = place & (COLUMNS - 1)
    high_ref[...] = column
    extra_ref[...] = place - owned
    column_rows = jnp.transpose(column.astype(f32))
    for g in range(groups):
        column_t[g] = column_rows[:, g * GROUP : (g + 1) * GROUP]

    def build(g, _):
        own = column_t[g].astype(bf16)
        numbers = lax.broadcasted_iota(i32, (slots, COLUMNS), 1).astype(f32).astype(bf16)
        rows8 = high_ref[pl.ds(pl.multiple_of(g * GROUP, GROUP), GROUP), :]
        for j in range(GROUP):
            n = g * GROUP + j
            onehot[n] = one_hot_rows(rows8[j : j + 1], COLUMNS)
            hit = numbers == own[:, j : j + 1]
            onehot_t[pl.ds(pl.multiple_of(n * slots, slots), slots), :] = jnp.where(
                hit, jnp.ones_like(numbers), jnp.zeros_like(numbers)
            )
        return 0

    lax.fori_loop(0, groups, build, 0)

    incoming[3].wait()
    stiff = stiff_ref[...]
    stiff_high[...] = stiff.astype(bf16)
    stiff_low[...] = (stiff - stiff_high[...].astype(f32)).astype(bf16)

    def gather(values):
        both = jnp.concatenate(split(values), axis=0)

        def step(g, _):
            low8 = low_ref[pl.ds(pl.multiple_of(g * GROUP, GROUP), GROUP), :]
            found = [[] for _ in range(components)]
            for j in range(GROUP):
                rows = pick_low(dot(both, onehot[g * GROUP + j]), low8[j : j + 1], components)
                for c in range(components):
                    found[c].append(rows[c])
            for c in range(components):
                at = pl.multiple_of(c * per_element + g * GROUP, GROUP)
                x_ref[pl.ds(at, GROUP), :] = jnp.concatenate(found[c], axis=0)
            return 0

        lax.fori_loop(0, groups, step, 0, unroll=UNROLL)

    def gather_interface(values):
        for side in range(slots // LANES):
            lanes = slice(side * LANES, (side + 1) * LANES)
            extra = extra_ref[:, lanes]
            lane_of = extra & (LANES - 1)
            piece_of = extra >> 7
            for c in range(components):
                rows = slice(c * per_element, (c + 1) * per_element)
                found = x_ref[rows, lanes]
                for piece in range(4 * face // LANES):
                    r = c * depth + own_rows + piece // 2
                    line = values[r : r + 1, (piece % 2) * LANES : (piece % 2 + 1) * LANES]
                    line = jnp.broadcast_to(line, (per_element, LANES))
                    taken = jnp.take_along_axis(line, lane_of, axis=1, mode="promise_in_bounds")
                    found = found + jnp.where(piece_of == piece, taken, 0.0)
                x_ref[rows, lanes] = found

    def scatter(values):
        y_ref[...] = values
        total_ref[...] = jnp.zeros_like(total_ref)

        def step(g, _):
            low8 = low_ref[pl.ds(pl.multiple_of(g * GROUP, GROUP), GROUP), :]
            parts = [
                y_ref[pl.ds(pl.multiple_of(c * per_element + g * GROUP, GROUP), GROUP), :]
                for c in range(components)
            ]
            wide = jnp.concatenate(
                [
                    spread_low([part[j : j + 1] for part in parts], low8[j : j + 1], depth)
                    for j in range(GROUP)
                ],
                axis=1,
            )
            at = pl.multiple_of(g * GROUP * slots, GROUP * slots)
            total_ref[...] += dot(wide, onehot_t[pl.ds(at, GROUP * slots), :])
            return 0

        lax.fori_loop(0, groups, step, 0, unroll=UNROLL)
        return total_ref[:height] + total_ref[height:]

    def products():
        x_high, x_low = split(x_ref[...])
        return dot(stiff_high[...], x_high) + (
            dot(stiff_low[...], x_high) + dot(stiff_high[...], x_low)
        )

    gather(start_table[...])
    gather_interface(receive_edge(field, 0))
    both = products()

    receive([near_copy(0), near_copy(1)])

    def far_finish(d, _):
        p = lax.rem(me + d, devices)
        far_copy(p, p).wait_recv()
        return 0

    lax.fori_loop(1, devices, far_finish, 0)
    records[...] = jnp.zeros_like(records)
    for p in range(devices):
        records[p : p + 1, :] = far_in[p]
    records[devices : devices + NEAR_CAP, :] = near_in[0]
    records[devices + NEAR_CAP : devices + 2 * NEAR_CAP, :] = near_in[1]
    got = records[...]
    slot_of = got[:, dofs + 2 : dofs + 3]
    aim = lax.broadcasted_iota(i32, (got.shape[0], slots), 1).astype(f32) + 1.0
    landing = jnp.where(aim == slot_of, 1.0, 0.0)
    arrived = jnp.dot(
        jnp.transpose(got), landing, precision=HIGHEST, preferred_element_type=f32
    )
    moved = jnp.where(staying, record, 0.0) + arrived
    loads = moved[:dofs]
    coefs = moved[dofs : dofs + 2]
    moved_loads_ref[...] = loads
    moved_coefs_ref[...] = coefs
    first, second = coefs[0:1], coefs[1:2]

    def element_values(both):
        return both[:dofs] * first + both[dofs:] * second

    on_diagonal = lax.broadcasted_iota(i32, (dofs, dofs), 0) == lax.broadcasted_iota(
        i32, (dofs, dofs), 1
    )
    diagonals = [
        jnp.sum(jnp.where(on_diagonal, stiff[k * dofs : (k + 1) * dofs], 0.0), axis=1, keepdims=True)
        for k in range(2)
    ]
    diagonal = scatter(diagonals[0] * first + diagonals[1] * second)
    send_edge(diagonal, 1)
    part = scatter(element_values(both) - loads)
    send_edge(part, 2)
    part_ref[...] = part
    diagonal = receive_edge(diagonal, 1)
    inverse_ref[...] = jnp.where(diagonal > 0.0, 1.0 / diagonal, 0.0)
    residual_ref[...] = jnp.zeros_like(residual_ref)
    update_ref[...] = jnp.zeros_like(update_ref)
    delta_ref[...] = jnp.zeros_like(delta_ref)
    weights = chebyshev_weights()
    table_row = lax.broadcasted_iota(i32, (height, COLUMNS), 0)
    is_owned = lax.rem(table_row, depth) < own_rows

    def next_update(part, old, new):
        residual = residual_ref[...] - part
        return residual, old * update_ref[...] + new * (residual * inverse_ref[...])

    def sweep_step(i, _):
        old, new = jnp.float32(0.0), jnp.float32(0.0)
        for k, (a, b) in enumerate(weights[:-1]):
            old = jnp.where(i == k, a, old)
            new = jnp.where(i == k, b, new)
        part = part_ref[...]
        gather(jnp.where(is_owned, next_update(part, old, new)[1], 0.0))
        residual, update = next_update(receive_edge(part, 2 + i), old, new)
        residual_ref[...] = residual
        update_ref[...] = update
        delta_ref[...] += update
        gather_interface(update)
        part = scatter(element_values(products()))
        send_edge(part, 3 + i)
        part_ref[...] = part
        return 0

    lax.fori_loop(0, len(weights) - 1, sweep_step, 0)

    part = receive_edge(part_ref[...], 1 + len(weights))
    delta = delta_ref[...] + next_update(part, *weights[-1])[1]
    result = start_table[...] + delta + move_faces(delta, 1, 0)
    for r in range(own_rows):
        for c in range(components):
            out_ref[c : c + 1, r * COLUMNS : (r + 1) * COLUMNS] = result[
                c * depth + r : c * depth + r + 1
            ]

    sent([near_copy(0), near_copy(1)])

    def far_sent(d, _):
        far_copy(lax.rem(me + d, devices), me).wait_send()
        return 0

    lax.fori_loop(1, devices, far_sent, 0)

    def edge_sent(t, _):
        sent([edge_copy(0, t), edge_copy(1, t)])
        return 0

    lax.fori_loop(0, edges, edge_sent, 0)


def local(
    devices, subs,
    start_field, element_loads, element_coefs, element_nodes, move_list, face_nodes, stiffness,
):
    dofs, slots = element_loads.shape
    per_element = element_nodes.shape[0]
    components = dofs // per_element
    owned = start_field.shape[1]
    face = face_nodes.shape[1]
    extra_rows = 4 * face // COLUMNS
    own_rows = owned // COLUMNS
    assert owned % COLUMNS == 0 and 4 * face == 3 * COLUMNS and own_rows % TILE + 3 <= TILE
    depth = -(-(own_rows + extra_rows) // TILE) * TILE
    table = (components * depth, COLUMNS)
    groups = per_element // GROUP
    rows = -(-(devices + 2 * NEAR_CAP) // LANES) * LANES
    edges = 2 + SWEEPS * DEGREE
    vmem = pl.BlockSpec(memory_space=pltpu.VMEM)
    smem = pl.BlockSpec(memory_space=pltpu.SMEM)
    anywhere = pl.BlockSpec(memory_space=pl.ANY)
    return pl.pallas_call(
        functools.partial(kernel, devices, subs),
        out_shape=(
            jax.ShapeDtypeStruct(start_field.shape, f32),
            jax.ShapeDtypeStruct((dofs, slots), f32),
            jax.ShapeDtypeStruct((2, slots), f32),
        ),
        in_specs=[anywhere, anywhere, vmem, anywhere, vmem, smem, vmem, anywhere],
        out_specs=(vmem, vmem, vmem),
        scratch_shapes=[
            pltpu.VMEM(start_field.shape, f32),
            pltpu.VMEM((dofs, slots), f32),
            pltpu.VMEM((per_element, slots), i32),
            pltpu.VMEM((2 * dofs, dofs), f32),
            pltpu.SemaphoreType.DMA((4,)),
            pltpu.VMEM((per_element, COLUMNS, slots), bf16),
            pltpu.VMEM((per_element * slots, COLUMNS), bf16),
            pltpu.VMEM((groups, slots, GROUP), f32),
            pltpu.VMEM((per_element, slots), i32),
            pltpu.VMEM((per_element, slots), i32),
            pltpu.VMEM((per_element, slots), i32),
            pltpu.VMEM((2 * dofs, dofs), bf16),
            pltpu.VMEM((2 * dofs, dofs), bf16),
            pltpu.VMEM((dofs, slots), f32),
            pltpu.VMEM((dofs, slots), f32),
            pltpu.VMEM(table, f32),
            pltpu.VMEM(table, f32),
            pltpu.VMEM(table, f32),
            pltpu.VMEM(table, f32),
            pltpu.VMEM(table, f32),
            pltpu.VMEM(table, f32),
            pltpu.VMEM((2 * table[0], COLUMNS), f32),
            pltpu.VMEM((devices, 1, slots), f32),
            pltpu.VMEM((devices, 1, slots), f32),
            pltpu.VMEM((2, NEAR_CAP, slots), f32),
            pltpu.VMEM((2, NEAR_CAP, slots), f32),
            pltpu.VMEM((rows, slots), f32),
            pltpu.VMEM((2, edges, components, TILE, LANES), f32),
            pltpu.VMEM((2, edges, components, TILE, LANES), f32),
            pltpu.SemaphoreType.DMA((devices,)),
            pltpu.SemaphoreType.DMA((devices,)),
            pltpu.SemaphoreType.DMA((2,)),
            pltpu.SemaphoreType.DMA((2,)),
            pltpu.SemaphoreType.DMA((2, edges)),
            pltpu.SemaphoreType.DMA((2, edges)),
        ],
        compiler_params=pltpu.CompilerParams(
            collective_id=0, has_side_effects=True, vmem_limit_bytes=56 * 1024 * 1024
        ),
        name="migrate_and_smooth",
    )(
        start_field,
        element_loads,
        element_coefs,
        element_nodes,
        move_list,
        face_nodes,
        face_nodes,
        stiffness.reshape(2 * dofs, dofs),
    )


def solution(mesh):
    devices = mesh.shape["seg"] * mesh.shape["sub"]
    return jax.shard_map(
        functools.partial(local, devices, mesh.shape["sub"]),
        mesh=mesh,
        in_specs=(
            P(None, ("seg", "sub")),
            P(None, ("seg", "sub")),
            P(None, ("seg", "sub")),
            P(None, ("seg", "sub")),
            P(None, ("seg", "sub")),
            P(None, ("seg", "sub")),
            P(),
        ),
        out_specs=(P(None, ("seg", "sub")), P(None, ("seg", "sub")), P(None, ("seg", "sub"))),
        check_vma=False,
    )
```
